512 devices in a mesh: section: 2 (over z_hi), ctx: 32 (over y, z_lo), tp: 8 (over x, core).
Axes of the slice: x: 4, y: 8, z: 8 (z_hi: 2, z_lo: 4; z = z_hi * 4 + z_lo), core: 2. Of those that a mesh axis runs over, the one named last changes fastest.
Arguments:
- inputs: bfloat16 [2, 4096, 8192], P('section', 'ctx', 'tp'), may hold values from -6 to 6
- kv_weight: bfloat16 [2, 8192, 1024], P('section', 'tp'), may hold values from -0.06629126 to 0.06629126
- queries_a: bfloat16 [2, 4096, 4096], P('section', 'ctx', 'tp'), may hold values from -160 to 160
- queries_b: bfloat16 [2, 4096, 4096], P('section', 'ctx', 'tp'), may hold values from -160 to 160
- grads_a: bfloat16 [2, 4096, 4096], P('section', 'ctx', 'tp'), may hold values from -6 to 6
- grads_b: bfloat16 [2, 4096, 4096], P('section', 'ctx', 'tp'), may hold values from -6 to 6
- span_order: int32 [64], replicated, may hold values from 0 to 63, each once
Outputs:
- out_a: bfloat16 [2, 4096, 4096], P('section', 'ctx', 'tp')
- out_b: bfloat16 [2, 4096, 4096], P('section', 'ctx', 'tp')
- grad_qa: bfloat16 [2, 4096, 4096], P('section', 'ctx', 'tp')
- grad_qb: bfloat16 [2, 4096, 4096], P('section', 'ctx', 'tp')
- grad_x: bfloat16 [2, 4096, 8192], P('section', 'ctx', 'tp')
The draws below stay inside these ranges and needn't reach their ends.
All inputs are finite; a program needn't handle non-finite values.
Results may differ from the reference program's by a relative error of at most 0.04.
The reference program's roundings to bfloat16 on the way count: a program that leaves them out, or rounds other values in their place, can miss the bound.
Values may be sent and summed in bfloat16 or wider, within the bound.
No kernel may reach another device: no remote copies, remote signals or barrier semaphores. Data moves between devices by JAX's collectives and lax.ppermute only.
A program may use at most 128 MiB of HBM per device.

```python
import jax
import jax.numpy as jnp
from jax import lax

D = 8192
HEADS = 32
KVH = 4
HD = 128
ROWS = 128
TOKENS = 4096
SPAN = 64
NSPAN = 64
GROUP = 8
HPD = 4
KV_DEV = 1
SHARE = 2
HPG = 4
N_CTX = 32
N_TP = 8


def base_inputs(key):
    inner = jax.random.fold_in(key, 101)
    values = jax.random.normal(jax.random.fold_in(inner, 3), (2, TOKENS, D), jnp.float32)
    return jnp.clip(values, -6.0, 6.0)


def base_weight(key):
    inner = jax.random.fold_in(key, 202)
    values = jax.random.normal(inner, (2, D, KVH * 2 * HD), jnp.float32)
    return jnp.clip(values, -6.0, 6.0) * D ** (-0.5)


def drawn_queries(key, salt):
    inner = jax.random.fold_in(key, salt)
    values = jnp.clip(2.5 * jax.random.normal(jax.random.fold_in(inner, 1), (2, TOKENS, HEADS * HD), jnp.float32), -15.0, 15.0)
    return jnp.clip(values, -160.0, 160.0)


def draw_inputs(key, part):
    return base_inputs(key).astype(jnp.bfloat16)


def draw_kv_weight(key, part):
    return base_weight(key).astype(jnp.bfloat16)


def draw_queries_a(key, part):
    return drawn_queries(key, 303).astype(jnp.bfloat16)


def draw_queries_b(key, part):
    return drawn_queries(key, 404).astype(jnp.bfloat16)


def shard_levels(key, extent, cuts, least, largest):
    factor_of, own = 1.0, jax.random.fold_in(key, 6)
    for axis_at, blocks in cuts:
        steps = jnp.exp(jax.random.uniform(jax.random.fold_in(own, axis_at), (blocks,), jnp.float32, least / len(cuts), largest / len(cuts)))
        factor_of = factor_of * jnp.repeat(steps, extent[axis_at] // blocks).reshape([-1 if axis == axis_at else 1 for axis in range(len(extent))])
    return factor_of


def centred(key, shape, deviation, bound, cuts=(), held_as=jnp.bfloat16):
    gain = shard_levels(key, shape, cuts, -0.22, 0.18) if cuts else 1.0
    values = jax.random.normal(key, shape, jnp.float32) * deviation * gain
    return jnp.minimum(jnp.maximum(values, -bound), bound).astype(held_as)


def setup_inputs(seed: int = 0) -> dict:
    keys = jax.random.split(jax.random.key(seed), 8)
    inputs = draw_inputs(jax.random.fold_in(keys[7], 71), 0)
    kv_weight = draw_kv_weight(jax.random.fold_in(keys[7], 71), 0)
    queries_a = draw_queries_a(jax.random.fold_in(keys[7], 71), 0)
    queries_b = draw_queries_b(jax.random.fold_in(keys[7], 71), 0)
    grads_a = centred(keys[4], (2, TOKENS, HEADS * HD), 1.0, 6.0, ((0, 2), (1, 32), (2, 8)))
    grads_b = centred(keys[5], (2, TOKENS, HEADS * HD), 1.0, 6.0, ((0, 2), (1, 32), (2, 8)))
    span_order = jax.random.permutation(keys[6], NSPAN).astype(jnp.int32)
    return {"inputs": inputs, "kv_weight": kv_weight, "queries_a": queries_a, "queries_b": queries_b, "grads_a": grads_a, "grads_b": grads_b, "span_order": span_order}


def rounded(value):
    return lax.optimization_barrier(value.astype(jnp.bfloat16)).astype(jnp.float32)


def token_positions(span_order):
    within = jnp.tile(jnp.arange(SPAN, dtype=jnp.int32), NSPAN)
    return jnp.repeat(span_order * SPAN, SPAN) + within


def one_layer(queries, keyvals, grads, positions):
    grouped = keyvals.reshape(TOKENS, KVH, 2, HD)
    score_scale = HD ** -0.5

    def per_device(tp_index):
        first_head = (tp_index * HPD) // GROUP
        chosen = lax.dynamic_slice_in_dim(grouped, first_head, KV_DEV, 1).astype(jnp.float32)
        key_heads = chosen[:, :, 0]
        value_heads = chosen[:, :, 1]
        query_heads = lax.dynamic_slice_in_dim(queries, tp_index * HPD * HD, HPD * HD, 1)
        query_heads = query_heads.astype(jnp.float32).reshape(TOKENS, KV_DEV, HPG, HD)
        grad_heads = lax.dynamic_slice_in_dim(grads, tp_index * HPD * HD, HPD * HD, 1)
        grad_heads = grad_heads.astype(jnp.float32).reshape(TOKENS, KV_DEV, HPG, HD)

        def shard(carry, shard_index):
            first_row = shard_index * ROWS
            query_rows = lax.dynamic_slice_in_dim(query_heads, first_row, ROWS, 0)
            grad_rows = lax.dynamic_slice_in_dim(grad_heads, first_row, ROWS, 0)
            pos_rows = lax.dynamic_slice_in_dim(positions, first_row, ROWS, 0)
            scores = jnp.einsum("rghe,tge->ghrt", query_rows, key_heads) * score_scale
            visible = positions[None, :] <= pos_rows[:, None]
            scores = jnp.where(visible, scores, -1e30)
            row_max = jnp.max(scores, axis=3, keepdims=True)
            weights = jnp.exp(scores - row_max)
            probabilities = rounded(weights / jnp.sum(weights, axis=3, keepdims=True))
            mixed = rounded(jnp.einsum("ghrt,tge->rghe", probabilities, value_heads))
            row_delta = jnp.sum(grad_rows * mixed, axis=3)
            row_delta = jnp.transpose(row_delta, (1, 2, 0))[..., None]
            grad_prob = jnp.einsum("rghe,tge->ghrt", grad_rows, value_heads)
            grad_score = rounded(probabilities * (grad_prob - row_delta))
            grad_query = jnp.einsum("ghrt,tge->rghe", grad_score, key_heads) * score_scale
            key_grad = jnp.einsum("ghrt,rghe->tge", grad_score, query_rows) * score_scale
            value_grad = jnp.einsum("ghrt,rghe->tge", probabilities, grad_rows)
            term = jnp.stack([key_grad, value_grad], axis=2)
            return carry + rounded(term), (mixed.astype(jnp.bfloat16), grad_query.astype(jnp.bfloat16))

        start_sum = jnp.zeros((TOKENS, KV_DEV, 2, HD), jnp.float32)
        total, (mixed, grad_query) = lax.scan(shard, start_sum, jnp.arange(N_CTX, dtype=jnp.int32))
        return (mixed.reshape(TOKENS, HPD * HD), grad_query.reshape(TOKENS, HPD * HD),
                total.reshape(TOKENS, KV_DEV * 2 * HD))

    mixed, grad_query, totals = lax.map(per_device, jnp.arange(N_TP, dtype=jnp.int32))
    mixed = jnp.transpose(mixed, (1, 0, 2)).reshape(TOKENS, HEADS * HD)
    grad_query = jnp.transpose(grad_query, (1, 0, 2)).reshape(TOKENS, HEADS * HD)
    return mixed, grad_query, totals


def reference(inputs, kv_weight, queries_a, queries_b, grads_a, grads_b, span_order):
    positions = token_positions(span_order)
    keyvals = [jnp.dot(inputs[pair_index], kv_weight[pair_index], preferred_element_type=jnp.float32).astype(jnp.bfloat16)
               for pair_index in range(2)]
    layers_a = [one_layer(queries_a[pair_index], keyvals[pair_index], grads_a[pair_index], positions)
                for pair_index in range(2)]
    layers_b = [one_layer(queries_b[section_index], keyvals[1 - section_index], grads_b[section_index], positions)
                for section_index in range(2)]
    grad_list = []
    for pair_index in range(2):
        section_sum = layers_a[pair_index][2] + layers_b[1 - pair_index][2]
        spread = jnp.transpose(section_sum, (1, 0, 2)).reshape(TOKENS, KVH, SHARE, 2 * HD)
        kv_grads = jnp.sum(spread, axis=2).astype(jnp.bfloat16).reshape(TOKENS, KVH * 2 * HD)
        grad_list.append(jnp.dot(kv_grads, kv_weight[pair_index].T, preferred_element_type=jnp.float32).astype(jnp.bfloat16))
    out_a = jnp.stack([layers_a[0][0], layers_a[1][0]])
    out_b = jnp.stack([layers_b[0][0], layers_b[1][0]])
    grad_qa = jnp.stack([layers_a[0][1], layers_a[1][1]])
    grad_qb = jnp.stack([layers_b[0][1], layers_b[1][1]])
    return (out_a, out_b, grad_qa, grad_qb, jnp.stack(grad_list))
```

```python
import math

import jax
import jax.numpy as jnp
from jax import lax
from jax.experimental import pallas as pl
from jax.experimental.pallas import tpu as pltpu
from jax.sharding import PartitionSpec as P

HEADS = 32
KVH = 4
HD = 128
SPAN = 64
N_SECTION = 2
N_Y = 8
N_Z = 4
N_CTX = 32
N_X = 4
N_CORE = 2
N_TP = 8
KEYS = N_CTX * SPAN * 2
ROWS = 128
HPD = 4
QROWS = HPD * ROWS
CHUNK = 512
NCHUNK = KEYS // CHUNK
EVERY = ("section", "ctx", "tp")
SCALE = HD ** (-0.5)
SCALE2 = SCALE * math.log2(math.e)
MIB = 1024 * 1024


def device_index(section, y, z, x, core):
    return (section * N_CTX + y * N_Z + z) * N_TP + x * N_CORE + core


def wide_groups():
    groups = []
    for section in range(N_SECTION):
        for x in range(N_X):
            for u in range(4):
                groups.append(
                    [device_index(section, u + 4 * w, z, x, 0) for w in range(2) for z in range(N_Z)]
                )
            for z in range(N_Z):
                groups.append([device_index(section, y, z, x, 1) for y in range(N_Y)])
    return groups


def narrow_groups():
    groups = []
    for section in range(N_SECTION):
        for x in range(N_X):
            for w in range(2):
                for z in range(N_Z):
                    groups.append([device_index(section, u + 4 * w, z, x, 0) for u in range(4)])
            for y in range(N_Y):
                groups.append([device_index(section, y, z, x, 1) for z in range(N_Z)])
    return groups


def block_owner(core):
    block = jnp.arange(N_CTX, dtype=jnp.int32)
    first, second = block // 8, block % 8
    owner_0 = (first + 4 * (second // 4)) * N_Z + second % 4
    owner_1 = second * N_Z + first
    return jnp.where(core == 0, owner_0, owner_1)


def swap_core(value):
    return lax.ppermute(value, "tp", [(i, i ^ 1) for i in range(N_TP)])


def swap_section(value):
    return lax.ppermute(value, "section", [(0, 1), (1, 0)])


def exchange(value, groups):
    return lax.all_to_all(value, EVERY, 0, 0, axis_index_groups=groups, tiled=True)


def project_kernel(x_ref, w_ref, o_ref):
    o_ref[0] = jnp.dot(x_ref[...], w_ref[...], preferred_element_type=jnp.float32)


def project(features, weight):
    return pl.pallas_call(
        project_kernel,
        grid=(KVH,),
        in_specs=[
            pl.BlockSpec((ROWS, 1024), lambda g: (0, 0)),
            pl.BlockSpec((1024, 2 * HD), lambda g: (0, g)),
        ],
        out_specs=pl.BlockSpec((1, ROWS, 2 * HD), lambda g: (g, 0, 0)),
        out_shape=jax.ShapeDtypeStruct((KVH, ROWS, 2 * HD), jnp.float32),
        name="kv_project",
    )(features, weight)


def unproject_kernel(g_ref, w_ref, o_ref):
    total = jnp.zeros((ROWS, 256), jnp.float32)
    for head in range(KVH):
        total += lax.dot_general(
            g_ref[head],
            w_ref[:, head * 256 : (head + 1) * 256],
            (((1,), (1,)), ((), ())),
            preferred_element_type=jnp.float32,
        )
    o_ref[...] = total.astype(jnp.bfloat16)


def unproject(kv_grads, weight):
    return pl.pallas_call(
        unproject_kernel,
        grid=(4,),
        in_specs=[
            pl.BlockSpec((KVH, ROWS, 2 * HD), lambda j: (0, 0, 0)),
            pl.BlockSpec((256, 1024), lambda j: (j, 0)),
        ],
        out_specs=pl.BlockSpec((ROWS, 256), lambda j: (0, j)),
        out_shape=jax.ShapeDtypeStruct((ROWS, 1024), jnp.bfloat16),
        name="kv_unproject",
    )(kv_grads, weight)


def nt(a, b):
    return lax.dot_general(a, b, (((1,), (1,)), ((), ())), preferred_element_type=jnp.float32)


def nn(a, b):
    return jnp.dot(a, b, preferred_element_type=jnp.float32)


def attention_kernel(
    base_ref, qa_ref, qgb_ref, ga_ref, own_ref, other_ref,
    oa_ref, gqa_ref, back_ref, gown_ref, gother_ref,
    q_s, g_s, kv_s, kt_s, vt_s, s_s, dk_s, dv_s,
):
    width = HPD * HD
    for head in range(HPD):
        cols = slice(head * HD, (head + 1) * HD)
        rows = slice(head * ROWS, (head + 1) * ROWS)
        q_s[0, rows, :] = qa_ref[:, cols]
        g_s[0, rows, :] = ga_ref[:, cols]
        q_s[1, rows, :] = qgb_ref[:, cols]
        g_s[1, rows, :] = qgb_ref[:, width + head * HD : width + (head + 1) * HD]
    half = KEYS // 2
    kv_s[:half, :] = own_ref[...]
    kv_s[half:, :] = other_ref[...]
    for c in range(NCHUNK):
        rows = slice(c * CHUNK, (c + 1) * CHUNK)
        kt_s[:, rows] = kv_s[rows, :HD].T
        vt_s[:, rows] = kv_s[rows, HD:].T

    lane = lax.broadcasted_iota(jnp.int32, (1, QROWS), 1) % ROWS
    q_pos = jnp.where(lane < SPAN, base_ref[64], base_ref[65]) + lane % SPAN
    key_row = lax.broadcasted_iota(jnp.int32, (SPAN, QROWS), 0)

    for unit in range(2):
        queries = q_s[unit]
        grads = g_s[unit]

        def scores(c, top):
            start = pl.multiple_of(c * CHUNK, CHUNK)
            tile = nt(kv_s[pl.ds(start, CHUNK), :HD], queries) * SCALE2
            for b in range(CHUNK // SPAN):
                base = base_ref[c * (CHUNK // SPAN) + b]
                part = jnp.where(
                    key_row <= q_pos - base, tile[b * SPAN : (b + 1) * SPAN], -1e30
                )
                s_s[pl.ds(start + b * SPAN, SPAN), :] = part
                top = jnp.maximum(top, jnp.max(part.reshape(SPAN // 8, 8, QROWS), axis=0))
            return top

        top = lax.fori_loop(0, NCHUNK, scores, jnp.full((8, QROWS), -1e30, jnp.float32))
        top = jnp.max(top, axis=0, keepdims=True)

        def mix(c, carry):
            total, out = carry
            start = pl.multiple_of(c * CHUNK, CHUNK)
            p = jnp.exp2(s_s[pl.ds(start, CHUNK), :] - top)
            total = total + jnp.sum(p.reshape(CHUNK // 8, 8, QROWS), axis=0)
            out = out + nn(vt_s[:, pl.ds(start, CHUNK)], p.astype(jnp.bfloat16))
            return total, out

        total, out = lax.fori_loop(
            0, NCHUNK, mix, (jnp.zeros((8, QROWS), jnp.float32), jnp.zeros((HD, QROWS), jnp.float32))
        )
        inverse = 1.0 / jnp.sum(total, axis=0, keepdims=True)
        mixed = (out * inverse).astype(jnp.bfloat16).astype(jnp.float32)
        delta = jnp.sum(mixed * grads.astype(jnp.float32).T, axis=0, keepdims=True)

        def back(c, grad_q):
            start = pl.multiple_of(c * CHUNK, CHUNK)
            rows = pl.ds(start, CHUNK)
            p = jnp.exp2(s_s[rows, :] - top) * inverse
            grad_p = nt(kv_s[rows, HD:], grads)
            grad_s = (p * (grad_p - delta)).astype(jnp.bfloat16)
            value_part = nn(p.astype(jnp.bfloat16), grads)
            key_part = nn(grad_s, queries)
            if unit == 0:
                dv_s[rows, :] = value_part
                dk_s[rows, :] = key_part
            else:
                dv_s[rows, :] += value_part
                dk_s[rows, :] += key_part
            return grad_q + nn(kt_s[:, rows], grad_s)

        grad_q = lax.fori_loop(0, NCHUNK, back, jnp.zeros((HD, QROWS), jnp.float32)) * SCALE
        for head in range(HPD):
            cols = slice(head * HD, (head + 1) * HD)
            lanes = slice(head * ROWS, (head + 1) * ROWS)
            o_head = mixed[:, lanes].T.astype(jnp.bfloat16)
            g_head = grad_q[:, lanes].T.astype(jnp.bfloat16)
            if unit == 0:
                oa_ref[:, cols] = o_head
                gqa_ref[:, cols] = g_head
            else:
                back_ref[:, cols] = o_head
                back_ref[:, width + head * HD : width + (head + 1) * HD] = g_head

    for ref, rows in ((gown_ref, slice(0, half)), (gother_ref, slice(half, KEYS))):
        ref[:, :HD] = (dk_s[rows, :] * SCALE).astype(jnp.bfloat16)
        ref[:, HD:] = dv_s[rows, :].astype(jnp.bfloat16)


def attention(bases, qa, qgb, ga, own, other):
    half = KEYS // 2
    bf = jnp.bfloat16
    whole = pl.BlockSpec(memory_space=pltpu.VMEM)
    return pl.pallas_call(
        attention_kernel,
        in_specs=[pl.BlockSpec(memory_space=pltpu.SMEM)] + [whole] * 5,
        out_specs=[whole] * 5,
        out_shape=[
            jax.ShapeDtypeStruct((ROWS, HPD * HD), bf),
            jax.ShapeDtypeStruct((ROWS, HPD * HD), bf),
            jax.ShapeDtypeStruct((ROWS, 2 * HPD * HD), bf),
            jax.ShapeDtypeStruct((half, 2 * HD), bf),
            jax.ShapeDtypeStruct((half, 2 * HD), bf),
        ],
        scratch_shapes=[
            pltpu.VMEM((2, QROWS, HD), bf),
            pltpu.VMEM((2, QROWS, HD), bf),
            pltpu.VMEM((KEYS, 2 * HD), bf),
            pltpu.VMEM((HD, KEYS), bf),
            pltpu.VMEM((HD, KEYS), bf),
            pltpu.VMEM((KEYS, QROWS), jnp.float32),
            pltpu.VMEM((KEYS, HD), jnp.float32),
            pltpu.VMEM((KEYS, HD), jnp.float32),
        ],
        compiler_params=pltpu.CompilerParams(vmem_limit_bytes=48 * MIB),
        cost_estimate=pl.CostEstimate(
            flops=24 * QROWS * KEYS * HD, bytes_accessed=6 * MIB, transcendentals=4 * QROWS * KEYS
        ),
        name="attention",
    )(bases, qa, qgb, ga, own, other)


def on_device(inputs, kv_weight, queries_a, queries_b, grads_a, grads_b, span_order):
    bf, f32 = jnp.bfloat16, jnp.float32
    weight = kv_weight[0]
    core = lax.axis_index("tp") % N_CORE
    ctx = lax.axis_index("ctx")
    wide, narrow = wide_groups(), narrow_groups()

    moved = swap_section(jnp.concatenate([queries_b[0], grads_b[0]], axis=1))

    partial = project(inputs[0], weight).reshape(N_TP * SPAN, 2 * HD)
    partial = lax.all_to_all(partial, "tp", 0, 0, tiled=True)
    own = jnp.sum(partial.reshape(N_TP, SPAN, 2 * HD), axis=0).astype(bf)

    own = exchange(jnp.broadcast_to(own[None], (8, SPAN, 2 * HD)), wide)
    own = exchange(jnp.broadcast_to(own[None], (4, 8, SPAN, 2 * HD)), narrow)
    own = own.reshape(N_CTX * SPAN, 2 * HD)
    other = swap_core(own)

    slots = jnp.concatenate(
        [2 * block_owner(core) + core, 2 * block_owner(1 - core) + 1 - core, 2 * ctx + jnp.arange(2)]
    )
    bases = span_order[slots] * SPAN

    out_a, grad_qa, back, grad_own, grad_other = attention(
        bases, queries_a[0], moved, grads_a[0], own, other
    )
    back = swap_section(back)
    grad_in = swap_core(grad_other)
    total = (grad_own.astype(f32) + grad_in.astype(f32)).astype(bf)
    total = exchange(total.reshape(4, 8, SPAN, 2 * HD), narrow)
    total = jnp.sum(total.astype(f32), axis=0).astype(bf)
    total = exchange(total, wide)
    total = jnp.sum(total.astype(f32), axis=0).astype(bf)
    total = lax.all_to_all(jnp.broadcast_to(total[None], (N_TP, SPAN, 2 * HD)), "tp", 0, 0, tiled=True)
    grad_x = unproject(total.reshape(KVH, ROWS, 2 * HD), weight)
    half = HPD * HD
    return (
        out_a[None],
        back[None, :, :half],
        grad_qa[None],
        back[None, :, half:],
        grad_x[None],
    )


def solution(mesh):
    split = P("section", "ctx", "tp")
    return jax.shard_map(
        on_device,
        mesh=mesh,
        in_specs=(split, P("section", "tp", None), split, split, split, split, P()),
        out_specs=(split,) * 5,
        check_vma=False,
    )
```

```python
import math

import jax
import jax.numpy as jnp
from jax import lax
from jax.experimental import pallas as pl
from jax.experimental.pallas import tpu as pltpu
from jax.sharding import PartitionSpec as P

HEADS = 32
KVH = 4
HD = 128
SPAN = 64
N_SECTION = 2
N_Y = 8
N_Z = 4
N_CTX = 32
N_X = 4
N_CORE = 2
N_TP = 8
KEYS = N_CTX * SPAN * 2
ROWS = 128
HPD = 4
QROWS = HPD * ROWS
CHUNK = 512
NCHUNK = KEYS // CHUNK
EVERY = ("section", "ctx", "tp")
SCALE = HD ** (-0.5)
SCALE2 = SCALE * math.log2(math.e)
MIB = 1024 * 1024


def device_index(section, y, z, x, core):
    return (section * N_CTX + y * N_Z + z) * N_TP + x * N_CORE + core


def wide_groups():
    groups = []
    for section in range(N_SECTION):
        for x in range(N_X):
            for u in range(4):
                groups.append(
                    [device_index(section, 2 * u + w, z, x, 0) for w in range(2) for z in range(N_Z)]
                )
            for z in range(N_Z):
                groups.append([device_index(section, y, z, x, 1) for y in range(N_Y)])
    return groups


def narrow_groups():
    groups = []
    for section in range(N_SECTION):
        for x in range(N_X):
            for w in range(2):
                for z in range(N_Z):
                    groups.append([device_index(section, 2 * u + w, z, x, 0) for u in range(4)])
            for y in range(N_Y):
                groups.append([device_index(section, y, z, x, 1) for z in range(N_Z)])
    return groups


def block_owner(core):
    block = jnp.arange(N_CTX, dtype=jnp.int32)
    first, second = block // 8, block % 8
    owner_0 = (2 * first + second // 4) * N_Z + second % 4
    owner_1 = second * N_Z + first
    return jnp.where(core == 0, owner_0, owner_1)


def swap_core(value):
    return lax.ppermute(value, "tp", [(i, i ^ 1) for i in range(N_TP)])


def swap_section(value):
    return lax.ppermute(value, "section", [(0, 1), (1, 0)])


def exchange(value, groups):
    return lax.all_to_all(value, EVERY, 0, 0, axis_index_groups=groups, tiled=True)


def project_kernel(x_ref, w_ref, o_ref):
    for g in range(KVH):
        o_ref[g] = nn(x_ref[...], w_ref[:, g * 2 * HD : (g + 1) * 2 * HD])


def project(features, weight):
    whole = pl.BlockSpec(memory_space=pltpu.VMEM)
    return pl.pallas_call(
        project_kernel,
        in_specs=[whole] * 2,
        out_specs=whole,
        out_shape=jax.ShapeDtypeStruct((KVH, ROWS, 2 * HD), jnp.float32),
        compiler_params=pltpu.CompilerParams(vmem_limit_bytes=16 * MIB),
        name="kv_project",
    )(features, weight)


def unproject_kernel(g_ref, w_ref, o_ref):
    total = nt(g_ref[0], w_ref[:, : 2 * HD])
    for g in range(1, KVH):
        total += nt(g_ref[g], w_ref[:, g * 2 * HD : (g + 1) * 2 * HD])
    o_ref[...] = total.astype(jnp.bfloat16)


def unproject(kv_grads, weight):
    whole = pl.BlockSpec(memory_space=pltpu.VMEM)
    return pl.pallas_call(
        unproject_kernel,
        in_specs=[whole] * 2,
        out_specs=whole,
        out_shape=jax.ShapeDtypeStruct((ROWS, weight.shape[0]), jnp.bfloat16),
        compiler_params=pltpu.CompilerParams(vmem_limit_bytes=16 * MIB),
        name="kv_unproject",
    )(kv_grads, weight)


def loop(body, carry):
    for c in range(NCHUNK):
        carry = body(c, carry)
    return carry


def nt(a, b):
    return lax.dot_general(a, b, (((1,), (1,)), ((), ())), preferred_element_type=jnp.float32)


def nn(a, b):
    return jnp.dot(a, b, preferred_element_type=jnp.float32)


def attention_kernel(
    base_ref, qa_ref, qb_ref, ga_ref, gb_ref, own_ref, other_ref,
    oa_ref, gqa_ref, back_ref, gown_ref, gother_ref,
    q_s, g_s, kv_s, kt_s, vt_s, s_s, dk_s, dv_s,
):
    for head in range(HPD):
        cols = slice(head * HD, (head + 1) * HD)
        rows = slice(head * ROWS, (head + 1) * ROWS)
        q_s[0, rows, :] = qa_ref[:, cols]
        g_s[0, rows, :] = ga_ref[:, cols]
        q_s[1, rows, :] = qb_ref[:, cols]
        g_s[1, rows, :] = gb_ref[:, cols]
    half = KEYS // 2
    kv_s[:half, :] = own_ref[...]
    kv_s[half:, :] = other_ref[...]
    for c in range(NCHUNK):
        rows = slice(c * CHUNK, (c + 1) * CHUNK)
        kt_s[:, rows] = kv_s[rows, :HD].T
        vt_s[:, rows] = kv_s[rows, HD:].T

    lane = lax.broadcasted_iota(jnp.int32, (1, QROWS), 1) % ROWS
    q_pos = jnp.where(lane < SPAN, base_ref[64], base_ref[65]) + lane % SPAN
    key_row = lax.broadcasted_iota(jnp.int32, (SPAN, QROWS), 0)

    for unit in range(2):
        queries = q_s[unit]
        grads = g_s[unit]

        def scores(c, top):
            start = c * CHUNK
            tile = nt(kv_s[pl.ds(start, CHUNK), :HD], queries) * SCALE2
            for b in range(CHUNK // SPAN):
                base = base_ref[c * (CHUNK // SPAN) + b]
                part = jnp.where(
                    key_row <= q_pos - base, tile[b * SPAN : (b + 1) * SPAN], -1e30
                )
                s_s[pl.ds(start + b * SPAN, SPAN), :] = part
                top = jnp.maximum(top, jnp.max(part.reshape(SPAN // 8, 8, QROWS), axis=0))
            return top

        top = loop(scores, jnp.full((8, QROWS), -1e30, jnp.float32))
        top = jnp.max(top, axis=0, keepdims=True)

        def mix(c, carry):
            total, out = carry
            start = c * CHUNK
            p = jnp.exp2(s_s[pl.ds(start, CHUNK), :] - top)
            total = total + jnp.sum(p.reshape(CHUNK // 8, 8, QROWS), axis=0)
            out = out + nn(vt_s[:, pl.ds(start, CHUNK)], p.astype(jnp.bfloat16))
            return total, out

        total, out = loop(mix, (jnp.zeros((8, QROWS), jnp.float32), jnp.zeros((HD, QROWS), jnp.float32))
        )
        inverse = 1.0 / jnp.sum(total, axis=0, keepdims=True)
        mixed = (out * inverse).astype(jnp.bfloat16).astype(jnp.float32)
        delta = jnp.sum(mixed * grads.astype(jnp.float32).T, axis=0, keepdims=True)

        def back(c, grad_q):
            start = c * CHUNK
            rows = pl.ds(start, CHUNK)
            p = jnp.exp2(s_s[rows, :] - top) * inverse
            grad_p = nt(kv_s[rows, HD:], grads)
            grad_s = (p * (grad_p - delta)).astype(jnp.bfloat16)
            value_part = nn(p.astype(jnp.bfloat16), grads)
            key_part = nn(grad_s, queries)
            if unit == 0:
                dv_s[rows, :] = value_part
                dk_s[rows, :] = key_part
            else:
                dv_s[rows, :] += value_part
                dk_s[rows, :] += key_part
            return grad_q + nn(kt_s[:, rows], grad_s)

        grad_q = loop(back, jnp.zeros((HD, QROWS), jnp.float32)) * SCALE
        for head in range(HPD):
            cols = slice(head * HD, (head + 1) * HD)
            lanes = slice(head * ROWS, (head + 1) * ROWS)
            o_head = mixed[:, lanes].T.astype(jnp.bfloat16)
            g_head = grad_q[:, lanes].T.astype(jnp.bfloat16)
            if unit == 0:
                oa_ref[:, cols] = o_head
                gqa_ref[:, cols] = g_head
            else:
                back_ref[:, cols] = o_head
                back_ref[:, QROWS + head * HD : QROWS + (head + 1) * HD] = g_head

    for ref, rows in ((gown_ref, slice(0, half)), (gother_ref, slice(half, KEYS))):
        ref[:, :HD] = (dk_s[rows, :] * SCALE).astype(jnp.bfloat16)
        ref[:, HD:] = dv_s[rows, :].astype(jnp.bfloat16)


def attention(bases, qa, qb, ga, gb, own, other):
    half = KEYS // 2
    bf = jnp.bfloat16
    whole = pl.BlockSpec(memory_space=pltpu.VMEM)
    return pl.pallas_call(
        attention_kernel,
        in_specs=[pl.BlockSpec(memory_space=pltpu.SMEM)] + [whole] * 6,
        out_specs=[whole] * 5,
        out_shape=[
            jax.ShapeDtypeStruct((ROWS, HPD * HD), bf),
            jax.ShapeDtypeStruct((ROWS, HPD * HD), bf),
            jax.ShapeDtypeStruct((ROWS, 2 * HPD * HD), bf),
            jax.ShapeDtypeStruct((half, 2 * HD), bf),
            jax.ShapeDtypeStruct((half, 2 * HD), bf),
        ],
        scratch_shapes=[
            pltpu.VMEM((2, QROWS, HD), bf),
            pltpu.VMEM((2, QROWS, HD), bf),
            pltpu.VMEM((KEYS, 2 * HD), bf),
            pltpu.VMEM((HD, KEYS), bf),
            pltpu.VMEM((HD, KEYS), bf),
            pltpu.VMEM((KEYS, QROWS), jnp.float32),
            pltpu.VMEM((KEYS, HD), jnp.float32),
            pltpu.VMEM((KEYS, HD), jnp.float32),
        ],
        compiler_params=pltpu.CompilerParams(vmem_limit_bytes=36 * MIB),
        cost_estimate=pl.CostEstimate(
            flops=24 * QROWS * KEYS * HD, bytes_accessed=6 * MIB, transcendentals=4 * QROWS * KEYS
        ),
        name="attention",
    )(bases, qa, qb, ga, gb, own, other)


def on_device(inputs, kv_weight, queries_a, queries_b, grads_a, grads_b, span_order):
    bf, f32 = jnp.bfloat16, jnp.float32
    weight = kv_weight[0]
    core = lax.axis_index("tp") % N_CORE
    ctx = lax.axis_index("ctx")
    wide, narrow = wide_groups(), narrow_groups()

    moved_q = swap_section(queries_b[0])
    moved_g = swap_section(grads_b[0])

    partial = project(inputs[0], weight)
    partial = lax.all_to_all(partial.reshape(N_TP, SPAN, 2 * HD), "tp", 0, 0, tiled=True)
    own = jnp.sum(partial, axis=0).astype(bf)

    own, moved_q = lax.optimization_barrier((own, moved_q))
    own = exchange(jnp.broadcast_to(own[None], (8, SPAN, 2 * HD)), wide)
    own, moved_g = lax.optimization_barrier((own, moved_g))
    own = exchange(jnp.broadcast_to(own[None], (4, 8, SPAN, 2 * HD)), narrow)
    own = own.reshape(N_CTX * SPAN, 2 * HD)
    other = swap_core(own)

    slots = jnp.concatenate(
        [2 * block_owner(core) + core, 2 * block_owner(1 - core) + 1 - core, 2 * ctx + jnp.arange(2)]
    )
    bases = span_order[slots] * SPAN

    out_a, grad_qa, back, grad_own, grad_other = attention(
        bases, queries_a[0], moved_q, grads_a[0], moved_g, own, other
    )
    back = swap_section(back)
    grad_in = swap_core(grad_other)
    total = (grad_own.astype(f32) + grad_in.astype(f32)).astype(bf)
    total = exchange(total.reshape(4, 8, SPAN, 2 * HD), narrow)
    total = jnp.sum(total.astype(f32), axis=0).astype(bf)
    total = exchange(total, wide)
    total = jnp.sum(total.astype(f32), axis=0).astype(bf)
    total = lax.all_to_all(jnp.broadcast_to(total[None], (N_TP, SPAN, 2 * HD)), "tp", 0, 0, tiled=True)
    grad_x = unproject(total.reshape(KVH, ROWS, 2 * HD), weight)
    half = HPD * HD
    return (
        out_a[None],
        back[None, :, :half],
        grad_qa[None],
        back[None, :, half:],
        grad_x[None],
    )


def solution(mesh):
    split = P("section", "ctx", "tp")
    return jax.shard_map(
        on_device,
        mesh=mesh,
        in_specs=(split, P("section", "tp", None), split, split, split, split, P()),
        out_specs=(split,) * 5,
        check_vma=False,
    )
```

```python
import math

import jax
import jax.numpy as jnp
from jax import lax
from jax.experimental import pallas as pl
from jax.experimental.pallas import tpu as pltpu
from jax.sharding import PartitionSpec as P

HEADS = 32
KVH = 4
HD = 128
SPAN = 64
N_SECTION = 2
N_Y = 8
N_Z = 4
N_CTX = 32
N_X = 4
N_CORE = 2
N_TP = 8
KEYS = N_CTX * SPAN * 2
ROWS = 128
HPD = 4
QROWS = HPD * ROWS
CHUNK = 512
NCHUNK = KEYS // CHUNK
EVERY = ("section", "ctx", "tp")
SCALE = HD ** (-0.5)
SCALE2 = SCALE * math.log2(math.e)
MIB = 1024 * 1024


def device_index(section, y, z, x, core):
    return (section * N_CTX + y * N_Z + z) * N_TP + x * N_CORE + core


def fold(u, w):
    return u + w * (N_Y - 1 - 2 * u)


def wide_groups():
    groups = []
    for section in range(N_SECTION):
        for x in range(N_X):
            for u in range(4):
                groups.append(
                    [device_index(section, fold(u, w), z, x, 0) for w in range(2) for z in range(N_Z)]
                )
            for z in range(N_Z):
                groups.append([device_index(section, y, z, x, 1) for y in range(N_Y)])
    return groups


def narrow_groups():
    groups = []
    for section in range(N_SECTION):
        for x in range(N_X):
            for w in range(2):
                for z in range(N_Z):
                    groups.append([device_index(section, fold(u, w), z, x, 0) for u in range(4)])
            for y in range(N_Y):
                groups.append([device_index(section, y, z, x, 1) for z in range(N_Z)])
    return groups


def block_owner(core):
    block = jnp.arange(N_CTX, dtype=jnp.int32)
    first, second = block // 8, block % 8
    owner_0 = fold(first, second // 4) * N_Z + second % 4
    owner_1 = second * N_Z + first
    return jnp.where(core == 0, owner_0, owner_1)


def swap_core(value):
    return lax.ppermute(value, "tp", [(i, i ^ 1) for i in range(N_TP)])


def swap_section(value):
    return lax.ppermute(value, "section", [(0, 1), (1, 0)])


def exchange(value, groups):
    return lax.all_to_all(value, EVERY, 0, 0, axis_index_groups=groups, tiled=True)


def project_kernel(x_ref, w_ref, o_ref):
    for g in range(KVH):
        o_ref[g] = nn(x_ref[...], w_ref[:, g * 2 * HD : (g + 1) * 2 * HD])


def project(features, weight):
    whole = pl.BlockSpec(memory_space=pltpu.VMEM)
    return pl.pallas_call(
        project_kernel,
        in_specs=[whole] * 2,
        out_specs=whole,
        out_shape=jax.ShapeDtypeStruct((KVH, ROWS, 2 * HD), jnp.float32),
        compiler_params=pltpu.CompilerParams(vmem_limit_bytes=16 * MIB),
        name="kv_project",
    )(features, weight)


def unproject_kernel(g_ref, w_ref, a_in, b_in, o_ref, a_out, b_out):
    a_out[...] = a_in[...]
    b_out[...] = b_in[...]
    total = nt(g_ref[0], w_ref[:, : 2 * HD])
    for g in range(1, KVH):
        total += nt(g_ref[g], w_ref[:, g * 2 * HD : (g + 1) * 2 * HD])
    o_ref[...] = total.astype(jnp.bfloat16)


def unproject(kv_grads, weight, out_b, grad_qb):
    whole = pl.BlockSpec(memory_space=pltpu.VMEM)
    return pl.pallas_call(
        unproject_kernel,
        in_specs=[whole] * 4,
        out_specs=[whole] * 3,
        out_shape=[
            jax.ShapeDtypeStruct((ROWS, weight.shape[0]), jnp.bfloat16),
            jax.ShapeDtypeStruct(out_b.shape, jnp.bfloat16),
            jax.ShapeDtypeStruct(grad_qb.shape, jnp.bfloat16),
        ],
        compiler_params=pltpu.CompilerParams(vmem_limit_bytes=16 * MIB),
        name="kv_unproject",
    )(kv_grads, weight, out_b, grad_qb)


def loop(body, carry):
    for c in range(NCHUNK):
        carry = body(c, carry)
    return carry


def nt(a, b):
    return lax.dot_general(a, b, (((1,), (1,)), ((), ())), preferred_element_type=jnp.float32)


def nn(a, b):
    return jnp.dot(a, b, preferred_element_type=jnp.float32)


def attention_kernel(
    base_ref, qa_ref, qb_ref, ga_ref, gb_ref, own_ref, other_ref,
    oa_ref, gqa_ref, ob_ref, gqb_ref, gown_ref, gother_ref,
    q_s, g_s, kv_s, kt_s, vt_s, s_s, dk_s, dv_s,
):
    for head in range(HPD):
        cols = slice(head * HD, (head + 1) * HD)
        rows = slice(head * ROWS, (head + 1) * ROWS)
        q_s[0, rows, :] = qa_ref[:, cols]
        g_s[0, rows, :] = ga_ref[:, cols]
        q_s[1, rows, :] = qb_ref[:, cols]
        g_s[1, rows, :] = gb_ref[:, cols]
    half = KEYS // 2
    kv_s[:half, :] = own_ref[...]
    kv_s[half:, :] = other_ref[...]
    for c in range(NCHUNK):
        rows = slice(c * CHUNK, (c + 1) * CHUNK)
        kt_s[:, rows] = kv_s[rows, :HD].T
        vt_s[:, rows] = kv_s[rows, HD:].T

    lane = lax.broadcasted_iota(jnp.int32, (1, QROWS), 1) % ROWS
    q_pos = jnp.where(lane < SPAN, base_ref[64], base_ref[65]) + lane % SPAN
    key_row = lax.broadcasted_iota(jnp.int32, (SPAN, QROWS), 0)

    for unit in range(2):
        queries = q_s[unit]
        grads = g_s[unit]

        def scores(c, top):
            start = c * CHUNK
            tile = nt(kv_s[pl.ds(start, CHUNK), :HD], queries) * SCALE2
            for b in range(CHUNK // SPAN):
                base = base_ref[c * (CHUNK // SPAN) + b]
                part = jnp.where(
                    key_row <= q_pos - base, tile[b * SPAN : (b + 1) * SPAN], -1e30
                )
                s_s[pl.ds(start + b * SPAN, SPAN), :] = part
                top = jnp.maximum(top, jnp.max(part.reshape(SPAN // 8, 8, QROWS), axis=0))
            return top

        top = loop(scores, jnp.full((8, QROWS), -1e30, jnp.float32))
        top = jnp.max(top, axis=0, keepdims=True)

        def mix(c, carry):
            total, out = carry
            start = c * CHUNK
            p = jnp.exp2(s_s[pl.ds(start, CHUNK), :] - top)
            total = total + jnp.sum(p.reshape(CHUNK // 8, 8, QROWS), axis=0)
            out = out + nn(vt_s[:, pl.ds(start, CHUNK)], p.astype(jnp.bfloat16))
            return total, out

        total, out = loop(mix, (jnp.zeros((8, QROWS), jnp.float32), jnp.zeros((HD, QROWS), jnp.float32))
        )
        inverse = 1.0 / jnp.sum(total, axis=0, keepdims=True)
        mixed = (out * inverse).astype(jnp.bfloat16).astype(jnp.float32)
        delta = jnp.sum(mixed * grads.astype(jnp.float32).T, axis=0, keepdims=True)

        def back(c, grad_q):
            start = c * CHUNK
            rows = pl.ds(start, CHUNK)
            p = jnp.exp2(s_s[rows, :] - top) * inverse
            grad_p = nt(kv_s[rows, HD:], grads)
            grad_s = (p * (grad_p - delta)).astype(jnp.bfloat16)
            value_part = nn(p.astype(jnp.bfloat16), grads)
            key_part = nn(grad_s, queries)
            if unit == 0:
                dv_s[rows, :] = value_part
                dk_s[rows, :] = key_part
            else:
                dv_s[rows, :] += value_part
                dk_s[rows, :] += key_part
            return grad_q + nn(kt_s[:, rows], grad_s)

        grad_q = loop(back, jnp.zeros((HD, QROWS), jnp.float32)) * SCALE
        for head in range(HPD):
            cols = slice(head * HD, (head + 1) * HD)
            lanes = slice(head * ROWS, (head + 1) * ROWS)
            o_head = mixed[:, lanes].T.astype(jnp.bfloat16)
            g_head = grad_q[:, lanes].T.astype(jnp.bfloat16)
            if unit == 0:
                oa_ref[:, cols] = o_head
                gqa_ref[:, cols] = g_head
            else:
                ob_ref[:, cols] = o_head
                gqb_ref[:, cols] = g_head

    for ref, rows in ((gown_ref, slice(0, half)), (gother_ref, slice(half, KEYS))):
        ref[:, :HD] = (dk_s[rows, :] * SCALE).astype(jnp.bfloat16)
        ref[:, HD:] = dv_s[rows, :].astype(jnp.bfloat16)


def attention(bases, qa, qb, ga, gb, own, other):
    half = KEYS // 2
    bf = jnp.bfloat16
    whole = pl.BlockSpec(memory_space=pltpu.VMEM)
    return pl.pallas_call(
        attention_kernel,
        in_specs=[pl.BlockSpec(memory_space=pltpu.SMEM)] + [whole] * 6,
        out_specs=[whole] * 6,
        out_shape=[
            jax.ShapeDtypeStruct((ROWS, HPD * HD), bf),
            jax.ShapeDtypeStruct((ROWS, HPD * HD), bf),
            jax.ShapeDtypeStruct((ROWS, HPD * HD), bf),
            jax.ShapeDtypeStruct((ROWS, HPD * HD), bf),
            jax.ShapeDtypeStruct((half, 2 * HD), bf),
            jax.ShapeDtypeStruct((half, 2 * HD), bf),
        ],
        scratch_shapes=[
            pltpu.VMEM((2, QROWS, HD), bf),
            pltpu.VMEM((2, QROWS, HD), bf),
            pltpu.VMEM((KEYS, 2 * HD), bf),
            pltpu.VMEM((HD, KEYS), bf),
            pltpu.VMEM((HD, KEYS), bf),
            pltpu.VMEM((KEYS, QROWS), jnp.float32),
            pltpu.VMEM((KEYS, HD), jnp.float32),
            pltpu.VMEM((KEYS, HD), jnp.float32),
        ],
        compiler_params=pltpu.CompilerParams(vmem_limit_bytes=28 * MIB),
        cost_estimate=pl.CostEstimate(
            flops=24 * QROWS * KEYS * HD, bytes_accessed=6 * MIB, transcendentals=4 * QROWS * KEYS
        ),
        name="attention",
    )(bases, qa, qb, ga, gb, own, other)


def on_device(inputs, kv_weight, queries_a, queries_b, grads_a, grads_b, span_order):
    bf, f32 = jnp.bfloat16, jnp.float32
    weight = kv_weight[0]
    core = lax.axis_index("tp") % N_CORE
    ctx = lax.axis_index("ctx")
    wide, narrow = wide_groups(), narrow_groups()

    moved_q = swap_section(queries_b[0])
    moved_g = swap_section(grads_b[0])

    partial = project(inputs[0], weight)
    partial = lax.all_to_all(partial.reshape(N_TP, SPAN, 2 * HD), "tp", 0, 0, tiled=True)
    own = jnp.sum(partial, axis=0).astype(bf)

    own, moved_q = lax.optimization_barrier((own, moved_q))
    own = exchange(jnp.broadcast_to(own[None], (8, SPAN, 2 * HD)), wide)
    own = exchange(jnp.broadcast_to(own[None], (4, 8, SPAN, 2 * HD)), narrow)
    own, moved_g = lax.optimization_barrier((own, moved_g))
    own = own.reshape(N_CTX * SPAN, 2 * HD)
    other = swap_core(own)

    slots = jnp.concatenate(
        [2 * block_owner(core) + core, 2 * block_owner(1 - core) + 1 - core, 2 * ctx + jnp.arange(2)]
    )
    bases = span_order[slots] * SPAN

    out_a, grad_qa, out_b, grad_qb, grad_own, grad_other = attention(
        bases, queries_a[0], moved_q, grads_a[0], moved_g, own, other
    )
    out_b = swap_section(out_b)
    grad_qb = swap_section(grad_qb)
    grad_in = swap_core(grad_other)
    total = (grad_own.astype(f32) + grad_in.astype(f32)).astype(bf)
    total = exchange(total.reshape(4, 8, SPAN, 2 * HD), narrow)
    total, out_b = lax.optimization_barrier((total, out_b))
    total = jnp.sum(total.astype(f32), axis=0).astype(bf)
    total = exchange(total, wide)
    total = jnp.sum(total.astype(f32), axis=0).astype(bf)
    total = lax.all_to_all(jnp.broadcast_to(total[None], (N_TP, SPAN, 2 * HD)), "tp", 0, 0, tiled=True)
    grad_x, out_b, grad_qb = unproject(
        total.reshape(KVH, ROWS, 2 * HD), weight, out_b, grad_qb
    )
    return out_a[None], out_b[None], grad_qa[None], grad_qb[None], grad_x[None]


def solution(mesh):
    split = P("section", "ctx", "tp")
    return jax.shard_map(
        on_device,
        mesh=mesh,
        in_specs=(split, P("section", "tp", None), split, split, split, split, P()),
        out_specs=(split,) * 5,
        check_vma=False,
    )
```

```python
import math

import jax
import jax.numpy as jnp
from jax import lax
from jax.experimental import pallas as pl
from jax.experimental.pallas import tpu as pltpu
from jax.sharding import PartitionSpec as P

HEADS = 32
KVH = 4
HD = 128
SPAN = 64
N_SECTION = 2
N_Y = 8
N_Z = 4
N_CTX = 32
N_X = 4
N_CORE = 2
N_TP = 8
KEYS = N_CTX * SPAN * 2
ROWS = 128
HPD = 4
QROWS = HPD * ROWS
CHUNK = 512
NCHUNK = KEYS // CHUNK
EVERY = ("section", "ctx", "tp")
SCALE = HD ** (-0.5)
SCALE2 = SCALE * math.log2(math.e)
MIB = 1024 * 1024


def device_index(section, y, z, x, core):
    return (section * N_CTX + y * N_Z + z) * N_TP + x * N_CORE + core


def fold(u, w):
    return u + w * (N_Y - 1 - 2 * u)


def wide_groups():
    groups = []
    for section in range(N_SECTION):
        for x in range(N_X):
            for u in range(4):
                groups.append(
                    [device_index(section, fold(u, w), z, x, 0) for w in range(2) for z in range(N_Z)]
                )
            for z in range(N_Z):
                groups.append([device_index(section, y, z, x, 1) for y in range(N_Y)])
    return groups


def narrow_groups():
    groups = []
    for section in range(N_SECTION):
        for x in range(N_X):
            for w in range(2):
                for z in range(N_Z):
                    groups.append([device_index(section, fold(u, w), z, x, 0) for u in range(4)])
            for y in range(N_Y):
                groups.append([device_index(section, y, z, x, 1) for z in range(N_Z)])
    return groups


def block_owner(core):
    block = jnp.arange(N_CTX, dtype=jnp.int32)
    first, second = block // 8, block % 8
    owner_0 = fold(first, second // 4) * N_Z + second % 4
    owner_1 = second * N_Z + first
    return jnp.where(core == 0, owner_0, owner_1)


def swap_core(value):
    return lax.ppermute(value, "tp", [(i, i ^ 1) for i in range(N_TP)])


def mirror(ctx):
    return ctx - ctx % N_Z + N_Z - 1 - ctx % N_Z


def swap_section(value):
    pairs = [
        (section * N_CTX + ctx, (1 - section) * N_CTX + mirror(ctx))
        for section in range(N_SECTION)
        for ctx in range(N_CTX)
    ]
    return lax.ppermute(value, ("section", "ctx"), pairs)


def exchange(value, groups):
    return lax.all_to_all(value, EVERY, 0, 0, axis_index_groups=groups, tiled=True)


def project_kernel(x_ref, w_ref, o_ref):
    for g in range(KVH):
        o_ref[g] = nn(x_ref[...], w_ref[:, g * 2 * HD : (g + 1) * 2 * HD])


def project(features, weight):
    whole = pl.BlockSpec(memory_space=pltpu.VMEM)
    return pl.pallas_call(
        project_kernel,
        in_specs=[whole] * 2,
        out_specs=whole,
        out_shape=jax.ShapeDtypeStruct((KVH, ROWS, 2 * HD), jnp.float32),
        compiler_params=pltpu.CompilerParams(vmem_limit_bytes=16 * MIB),
        name="kv_project",
    )(features, weight)


def unproject_kernel(g_ref, w_ref, back_ref, o_ref, a_out, b_out):
    a_out[...] = back_ref[:, :QROWS]
    b_out[...] = back_ref[:, QROWS:]
    total = nt(g_ref[0], w_ref[:, : 2 * HD])
    for g in range(1, KVH):
        total += nt(g_ref[g], w_ref[:, g * 2 * HD : (g + 1) * 2 * HD])
    o_ref[...] = total.astype(jnp.bfloat16)


def unproject(kv_grads, weight, back):
    whole = pl.BlockSpec(memory_space=pltpu.VMEM)
    return pl.pallas_call(
        unproject_kernel,
        in_specs=[whole] * 3,
        out_specs=[whole] * 3,
        out_shape=[
            jax.ShapeDtypeStruct((ROWS, weight.shape[0]), jnp.bfloat16),
            jax.ShapeDtypeStruct((ROWS, QROWS), jnp.bfloat16),
            jax.ShapeDtypeStruct((ROWS, QROWS), jnp.bfloat16),
        ],
        compiler_params=pltpu.CompilerParams(vmem_limit_bytes=16 * MIB),
        name="kv_unproject",
    )(kv_grads, weight, back)


def loop(body, carry):
    for c in range(NCHUNK):
        carry = body(c, carry)
    return carry


def nt(a, b):
    return lax.dot_general(a, b, (((1,), (1,)), ((), ())), preferred_element_type=jnp.float32)


def nn(a, b):
    return jnp.dot(a, b, preferred_element_type=jnp.float32)


def attention_kernel(
    base_ref, qa_ref, qb_ref, ga_ref, gb_ref, own_ref, other_ref,
    oa_ref, gqa_ref, back_ref, gown_ref, gother_ref,
    q_s, g_s, kv_s, kt_s, vt_s, s_s, dk_s, dv_s,
):
    for head in range(HPD):
        cols = slice(head * HD, (head + 1) * HD)
        rows = slice(head * ROWS, (head + 1) * ROWS)
        q_s[0, rows, :] = qa_ref[:, cols]
        g_s[0, rows, :] = ga_ref[:, cols]
        q_s[1, rows, :] = qb_ref[:, cols]
        g_s[1, rows, :] = gb_ref[:, cols]
    half = KEYS // 2
    kv_s[:half, :] = own_ref[...]
    kv_s[half:, :] = other_ref[...]
    for c in range(NCHUNK):
        rows = slice(c * CHUNK, (c + 1) * CHUNK)
        kt_s[:, rows] = kv_s[rows, :HD].T
        vt_s[:, rows] = kv_s[rows, HD:].T

    lane = lax.broadcasted_iota(jnp.int32, (1, QROWS), 1) % ROWS
    key_row = lax.broadcasted_iota(jnp.int32, (SPAN, QROWS), 0)

    for unit in range(2):
        queries = q_s[unit]
        grads = g_s[unit]
        q_pos = jnp.where(lane < SPAN, base_ref[64 + 2 * unit], base_ref[65 + 2 * unit]) + lane % SPAN

        def scores(c, top):
            start = c * CHUNK
            tile = nt(kv_s[pl.ds(start, CHUNK), :HD], queries) * SCALE2
            for b in range(CHUNK // SPAN):
                base = base_ref[c * (CHUNK // SPAN) + b]
                part = jnp.where(
                    key_row <= q_pos - base, tile[b * SPAN : (b + 1) * SPAN], -1e30
                )
                s_s[pl.ds(start + b * SPAN, SPAN), :] = part
                top = jnp.maximum(top, jnp.max(part.reshape(SPAN // 8, 8, QROWS), axis=0))
            return top

        top = loop(scores, jnp.full((8, QROWS), -1e30, jnp.float32))
        top = jnp.max(top, axis=0, keepdims=True)

        def mix(c, carry):
            total, out = carry
            start = c * CHUNK
            p = jnp.exp2(s_s[pl.ds(start, CHUNK), :] - top)
            total = total + jnp.sum(p.reshape(CHUNK // 8, 8, QROWS), axis=0)
            out = out + nn(vt_s[:, pl.ds(start, CHUNK)], p.astype(jnp.bfloat16))
            return total, out

        total, out = loop(mix, (jnp.zeros((8, QROWS), jnp.float32), jnp.zeros((HD, QROWS), jnp.float32))
        )
        inverse = 1.0 / jnp.sum(total, axis=0, keepdims=True)
        mixed = (out * inverse).astype(jnp.bfloat16).astype(jnp.float32)
        delta = jnp.sum(mixed * grads.astype(jnp.float32).T, axis=0, keepdims=True)

        def back(c, grad_q):
            start = c * CHUNK
            rows = pl.ds(start, CHUNK)
            p = jnp.exp2(s_s[rows, :] - top) * inverse
            grad_p = nt(kv_s[rows, HD:], grads)
            grad_s = (p * (grad_p - delta)).astype(jnp.bfloat16)
            value_part = nn(p.astype(jnp.bfloat16), grads)
            key_part = nn(grad_s, queries)
            if unit == 0:
                dv_s[rows, :] = value_part
                dk_s[rows, :] = key_part
            else:
                dv_s[rows, :] += value_part
                dk_s[rows, :] += key_part
            return grad_q + nn(kt_s[:, rows], grad_s)

        grad_q = loop(back, jnp.zeros((HD, QROWS), jnp.float32)) * SCALE
        for head in range(HPD):
            cols = slice(head * HD, (head + 1) * HD)
            lanes = slice(head * ROWS, (head + 1) * ROWS)
            o_head = mixed[:, lanes].T.astype(jnp.bfloat16)
            g_head = grad_q[:, lanes].T.astype(jnp.bfloat16)
            if unit == 0:
                oa_ref[:, cols] = o_head
                gqa_ref[:, cols] = g_head
            else:
                back_ref[:, cols] = o_head
                back_ref[:, QROWS + head * HD : QROWS + (head + 1) * HD] = g_head

    for ref, rows in ((gown_ref, slice(0, half)), (gother_ref, slice(half, KEYS))):
        ref[:, :HD] = (dk_s[rows, :] * SCALE).astype(jnp.bfloat16)
        ref[:, HD:] = dv_s[rows, :].astype(jnp.bfloat16)


def attention(bases, qa, qb, ga, gb, own, other):
    half = KEYS // 2
    bf = jnp.bfloat16
    whole = pl.BlockSpec(memory_space=pltpu.VMEM)
    return pl.pallas_call(
        attention_kernel,
        in_specs=[pl.BlockSpec(memory_space=pltpu.SMEM)] + [whole] * 6,
        out_specs=[whole] * 5,
        out_shape=[
            jax.ShapeDtypeStruct((ROWS, HPD * HD), bf),
            jax.ShapeDtypeStruct((ROWS, HPD * HD), bf),
            jax.ShapeDtypeStruct((ROWS, 2 * HPD * HD), bf),
            jax.ShapeDtypeStruct((half, 2 * HD), bf),
            jax.ShapeDtypeStruct((half, 2 * HD), bf),
        ],
        scratch_shapes=[
            pltpu.VMEM((2, QROWS, HD), bf),
            pltpu.VMEM((2, QROWS, HD), bf),
            pltpu.VMEM((KEYS, 2 * HD), bf),
            pltpu.VMEM((HD, KEYS), bf),
            pltpu.VMEM((HD, KEYS), bf),
            pltpu.VMEM((KEYS, QROWS), jnp.float32),
            pltpu.VMEM((KEYS, HD), jnp.float32),
            pltpu.VMEM((KEYS, HD), jnp.float32),
        ],
        compiler_params=pltpu.CompilerParams(vmem_limit_bytes=28 * MIB),
        cost_estimate=pl.CostEstimate(
            flops=24 * QROWS * KEYS * HD, bytes_accessed=6 * MIB, transcendentals=4 * QROWS * KEYS
        ),
        name="attention",
    )(bases, qa, qb, ga, gb, own, other)


def on_device(inputs, kv_weight, queries_a, queries_b, grads_a, grads_b, span_order):
    bf, f32 = jnp.bfloat16, jnp.float32
    weight = kv_weight[0]
    core = lax.axis_index("tp") % N_CORE
    ctx = lax.axis_index("ctx")
    wide, narrow = wide_groups(), narrow_groups()

    moved_q = swap_section(queries_b[0])
    moved_g = swap_section(grads_b[0])

    partial = project(inputs[0], weight)
    partial = lax.all_to_all(partial.reshape(N_TP, SPAN, 2 * HD), "tp", 0, 0, tiled=True)
    own = jnp.sum(partial, axis=0).astype(bf)

    own, moved_q = lax.optimization_barrier((own, moved_q))
    own = exchange(jnp.broadcast_to(own[None], (8, SPAN, 2 * HD)), wide)
    own = exchange(jnp.broadcast_to(own[None], (4, 8, SPAN, 2 * HD)), narrow)
    own, moved_g = lax.optimization_barrier((own, moved_g))
    own = own.reshape(N_CTX * SPAN, 2 * HD)
    other = swap_core(own)

    slots = jnp.concatenate(
        [2 * block_owner(core) + core, 2 * block_owner(1 - core) + 1 - core, 2 * ctx + jnp.arange(2), 2 * mirror(ctx) + jnp.arange(2)]
    )
    bases = span_order[slots] * SPAN

    out_a, grad_qa, back, grad_own, grad_other = attention(
        bases, queries_a[0], moved_q, grads_a[0], moved_g, own, other
    )
    back = swap_section(back)
    grad_in = swap_core(grad_other)
    total = (grad_own.astype(f32) + grad_in.astype(f32)).astype(bf)
    total = exchange(total.reshape(4, 8, SPAN, 2 * HD), narrow)
    total, back = lax.optimization_barrier((total, back))
    total = jnp.sum(total.astype(f32), axis=0).astype(bf)
    total = exchange(total, wide)
    total = jnp.sum(total.astype(f32), axis=0).astype(bf)
    total = lax.all_to_all(jnp.broadcast_to(total[None], (N_TP, SPAN, 2 * HD)), "tp", 0, 0, tiled=True)
    grad_x, out_b, grad_qb = unproject(
        total.reshape(KVH, ROWS, 2 * HD), weight, back
    )
    return out_a[None], out_b[None], grad_qa[None], grad_qb[None], grad_x[None]


def solution(mesh):
    split = P("section", "ctx", "tp")
    return jax.shard_map(
        on_device,
        mesh=mesh,
        in_specs=(split, P("section", "tp", None), split, split, split, split, P()),
        out_specs=(split,) * 5,
        check_vma=False,
    )
```

```python
import math

import jax
import jax.numpy as jnp
from jax import lax
from jax.experimental import pallas as pl
from jax.experimental.pallas import tpu as pltpu
from jax.sharding import PartitionSpec as P

HEADS = 32
KVH = 4
HD = 128
SPAN = 64
N_SECTION = 2
N_Y = 8
N_Z = 4
N_CTX = 32
N_X = 4
N_CORE = 2
N_TP = 8
KEYS = N_CTX * SPAN * 2
ROWS = 128
HPD = 4
QROWS = HPD * ROWS
ALLROWS = 2 * QROWS
CHUNK = 512
NCHUNK = KEYS // CHUNK
EVERY = ("section", "ctx", "tp")
SCALE = HD ** (-0.5)
SCALE2 = SCALE * math.log2(math.e)
MIB = 1024 * 1024


def device_index(section, y, z, x, core):
    return (section * N_CTX + y * N_Z + z) * N_TP + x * N_CORE + core


def fold(u, w):
    return u + w * (N_Y - 1 - 2 * u)


def wide_groups():
    groups = []
    for section in range(N_SECTION):
        for x in range(N_X):
            for u in range(4):
                groups.append(
                    [device_index(section, fold(u, w), z, x, 0) for w in range(2) for z in range(N_Z)]
                )
            for z in range(N_Z):
                groups.append([device_index(section, y, z, x, 1) for y in range(N_Y)])
    return groups


def narrow_groups():
    groups = []
    for section in range(N_SECTION):
        for x in range(N_X):
            for w in range(2):
                for z in range(N_Z):
                    groups.append([device_index(section, fold(u, w), z, x, 0) for u in range(4)])
            for y in range(N_Y):
                groups.append([device_index(section, y, z, x, 1) for z in range(N_Z)])
    return groups


def block_owner(core):
    block = jnp.arange(N_CTX, dtype=jnp.int32)
    first, second = block // 8, block % 8
    owner_0 = fold(first, second // 4) * N_Z + second % 4
    owner_1 = second * N_Z + first
    return jnp.where(core == 0, owner_0, owner_1)


def swap_core(value):
    return lax.ppermute(value, "tp", [(i, i ^ 1) for i in range(N_TP)])


def mirror(ctx):
    return ctx - ctx % N_Z + N_Z - 1 - ctx % N_Z


def swap_section(value):
    pairs = [
        (section * N_CTX + ctx, (1 - section) * N_CTX + mirror(ctx))
        for section in range(N_SECTION)
        for ctx in range(N_CTX)
    ]
    return lax.ppermute(value, ("section", "ctx"), pairs)


def exchange(value, groups):
    return lax.all_to_all(value, EVERY, 0, 0, axis_index_groups=groups, tiled=True)


def project_kernel(x_ref, w_ref, o_ref):
    for g in range(KVH):
        o_ref[g] = nn(x_ref[...], w_ref[:, g * 2 * HD : (g + 1) * 2 * HD])


def project(features, weight):
    whole = pl.BlockSpec(memory_space=pltpu.VMEM)
    return pl.pallas_call(
        project_kernel,
        in_specs=[whole] * 2,
        out_specs=whole,
        out_shape=jax.ShapeDtypeStruct((KVH, ROWS, 2 * HD), jnp.float32),
        compiler_params=pltpu.CompilerParams(vmem_limit_bytes=16 * MIB),
        name="kv_project",
    )(features, weight)


def unproject_kernel(g_ref, w_ref, a_in, b_in, o_ref, a_out, b_out):
    a_out[...] = a_in[...]
    b_out[...] = b_in[...]
    total = nt(g_ref[0], w_ref[:, : 2 * HD])
    for g in range(1, KVH):
        total += nt(g_ref[g], w_ref[:, g * 2 * HD : (g + 1) * 2 * HD])
    o_ref[...] = total.astype(jnp.bfloat16)


def unproject(kv_grads, weight, out_b, grad_qb):
    whole = pl.BlockSpec(memory_space=pltpu.VMEM)
    return pl.pallas_call(
        unproject_kernel,
        in_specs=[whole] * 4,
        out_specs=[whole] * 3,
        out_shape=[
            jax.ShapeDtypeStruct((ROWS, weight.shape[0]), jnp.bfloat16),
            jax.ShapeDtypeStruct((ROWS, QROWS), jnp.bfloat16),
            jax.ShapeDtypeStruct((ROWS, QROWS), jnp.bfloat16),
        ],
        compiler_params=pltpu.CompilerParams(vmem_limit_bytes=16 * MIB),
        name="kv_unproject",
    )(kv_grads, weight, out_b, grad_qb)


def nt(a, b):
    return lax.dot_general(a, b, (((1,), (1,)), ((), ())), preferred_element_type=jnp.float32)


def nn(a, b):
    return jnp.dot(a, b, preferred_element_type=jnp.float32)


def attention_kernel(
    base_ref, qa_ref, qb_ref, ga_ref, gb_ref, own_ref, other_ref,
    oa_ref, gqa_ref, ob_ref, gqb_ref, gown_ref, gother_ref,
    q_s, g_s, kt_s, vt_s, s_s,
):
    for head in range(HPD):
        cols = slice(head * HD, (head + 1) * HD)
        rows_a = slice(head * ROWS, (head + 1) * ROWS)
        rows_b = slice(QROWS + head * ROWS, QROWS + (head + 1) * ROWS)
        q_s[rows_a, :] = qa_ref[:, cols]
        g_s[rows_a, :] = ga_ref[:, cols]
        q_s[rows_b, :] = qb_ref[:, cols]
        g_s[rows_b, :] = gb_ref[:, cols]
    queries = q_s[...]
    grads = g_s[...]

    def key_rows(c):
        ref = own_ref if c < NCHUNK // 2 else other_ref
        return ref, slice(c % (NCHUNK // 2) * CHUNK, (c % (NCHUNK // 2) + 1) * CHUNK)

    lane = lax.broadcasted_iota(jnp.int32, (1, ALLROWS), 1)
    row = lane % ROWS
    base_a = jnp.where(row < SPAN, base_ref[64], base_ref[65])
    base_b = jnp.where(row < SPAN, base_ref[66], base_ref[67])
    q_pos = jnp.where(lane < QROWS, base_a, base_b) + row % SPAN
    key_row = lax.broadcasted_iota(jnp.int32, (SPAN, ALLROWS), 0)

    top = jnp.full((8, ALLROWS), -1e30, jnp.float32)
    for c in range(NCHUNK):
        ref, rows = key_rows(c)
        start = c * CHUNK
        tile = nt(ref[rows, :HD], queries) * SCALE2
        kt_s[:, start : start + CHUNK] = ref[rows, :HD].T
        vt_s[:, start : start + CHUNK] = ref[rows, HD:].T
        for b in range(CHUNK // SPAN):
            base = base_ref[c * (CHUNK // SPAN) + b]
            part = jnp.where(key_row <= q_pos - base, tile[b * SPAN : (b + 1) * SPAN], -1e30)
            s_s[start + b * SPAN : start + (b + 1) * SPAN, :] = part
            top = jnp.maximum(top, jnp.max(part.reshape(SPAN // 8, 8, ALLROWS), axis=0))
    top = jnp.max(top, axis=0, keepdims=True)

    total = jnp.zeros((8, ALLROWS), jnp.float32)
    out = jnp.zeros((HD, ALLROWS), jnp.float32)
    for c in range(NCHUNK):
        start = c * CHUNK
        p = jnp.exp2(s_s[start : start + CHUNK, :] - top)
        total = total + jnp.sum(p.reshape(CHUNK // 8, 8, ALLROWS), axis=0)
        out = out + nn(vt_s[:, start : start + CHUNK], p.astype(jnp.bfloat16))
    inverse = 1.0 / jnp.sum(total, axis=0, keepdims=True)
    mixed = (out * inverse).astype(jnp.bfloat16).astype(jnp.float32)
    delta = jnp.sum(mixed * grads.astype(jnp.float32).T, axis=0, keepdims=True)

    grad_q = jnp.zeros((HD, ALLROWS), jnp.float32)
    for c in range(NCHUNK):
        ref, rows = key_rows(c)
        grad_ref = gown_ref if c < NCHUNK // 2 else gother_ref
        start = c * CHUNK
        p = jnp.exp2(s_s[start : start + CHUNK, :] - top) * inverse
        grad_p = nt(ref[rows, HD:], grads)
        grad_s = (p * (grad_p - delta)).astype(jnp.bfloat16)
        grad_ref[rows, HD:] = nn(p.astype(jnp.bfloat16), grads).astype(jnp.bfloat16)
        grad_ref[rows, :HD] = (nn(grad_s, queries) * SCALE).astype(jnp.bfloat16)
        grad_q = grad_q + nn(kt_s[:, start : start + CHUNK], grad_s)
    grad_q = grad_q * SCALE

    for head in range(HPD):
        cols = slice(head * HD, (head + 1) * HD)
        for first, o_ref, g_ref in ((0, oa_ref, gqa_ref), (QROWS, ob_ref, gqb_ref)):
            lanes = slice(first + head * ROWS, first + (head + 1) * ROWS)
            o_ref[:, cols] = mixed[:, lanes].T.astype(jnp.bfloat16)
            g_ref[:, cols] = grad_q[:, lanes].T.astype(jnp.bfloat16)


def attention(bases, qa, qb, ga, gb, own, other):
    half = KEYS // 2
    bf = jnp.bfloat16
    whole = pl.BlockSpec(memory_space=pltpu.VMEM)
    return pl.pallas_call(
        attention_kernel,
        in_specs=[pl.BlockSpec(memory_space=pltpu.SMEM)] + [whole] * 6,
        out_specs=[whole] * 6,
        out_shape=[
            jax.ShapeDtypeStruct((ROWS, HPD * HD), bf),
            jax.ShapeDtypeStruct((ROWS, HPD * HD), bf),
            jax.ShapeDtypeStruct((ROWS, HPD * HD), bf),
            jax.ShapeDtypeStruct((ROWS, HPD * HD), bf),
            jax.ShapeDtypeStruct((half, 2 * HD), bf),
            jax.ShapeDtypeStruct((half, 2 * HD), bf),
        ],
        scratch_shapes=[
            pltpu.VMEM((ALLROWS, HD), bf),
            pltpu.VMEM((ALLROWS, HD), bf),
            pltpu.VMEM((HD, KEYS), bf),
            pltpu.VMEM((HD, KEYS), bf),
            pltpu.VMEM((KEYS, ALLROWS), jnp.float32),
        ],
        compiler_params=pltpu.CompilerParams(vmem_limit_bytes=34 * MIB),
        cost_estimate=pl.CostEstimate(
            flops=24 * QROWS * KEYS * HD, bytes_accessed=6 * MIB, transcendentals=4 * QROWS * KEYS
        ),
        name="attention",
    )(bases, qa, qb, ga, gb, own, other)


def on_device(inputs, kv_weight, queries_a, queries_b, grads_a, grads_b, span_order):
    bf, f32 = jnp.bfloat16, jnp.float32
    weight = kv_weight[0]
    core = lax.axis_index("tp") % N_CORE
    ctx = lax.axis_index("ctx")
    wide, narrow = wide_groups(), narrow_groups()

    moved_q = swap_section(queries_b[0])
    moved_g = swap_section(grads_b[0])

    partial = project(inputs[0], weight)
    partial = lax.all_to_all(partial.reshape(N_TP, SPAN, 2 * HD), "tp", 0, 0, tiled=True)
    own = jnp.sum(partial, axis=0).astype(bf)

    own = exchange(jnp.broadcast_to(own[None], (8, SPAN, 2 * HD)), wide)
    own, moved_q = lax.optimization_barrier((own, moved_q))
    own = exchange(jnp.broadcast_to(own[None], (4, 8, SPAN, 2 * HD)), narrow)
    own, moved_g = lax.optimization_barrier((own, moved_g))
    own = own.reshape(N_CTX * SPAN, 2 * HD)
    other = swap_core(own)

    slots = jnp.concatenate(
        [2 * block_owner(core) + core, 2 * block_owner(1 - core) + 1 - core, 2 * ctx + jnp.arange(2), 2 * mirror(ctx) + jnp.arange(2)]
    )
    bases = span_order[slots] * SPAN

    out_a, grad_qa, out_b, grad_qb, grad_own, grad_other = attention(
        bases, queries_a[0], moved_q, grads_a[0], moved_g, own, other
    )
    out_b = swap_section(out_b)
    grad_qb = swap_section(grad_qb)
    grad_in = swap_core(grad_other)
    total = (grad_own.astype(f32) + grad_in.astype(f32)).astype(bf)
    total = exchange(total.reshape(4, 8, SPAN, 2 * HD), narrow)
    total, out_b = lax.optimization_barrier((total, out_b))
    total = jnp.sum(total.astype(f32), axis=0).astype(bf)
    total = exchange(total, wide)
    total, grad_qb = lax.optimization_barrier((total, grad_qb))
    total = jnp.sum(total.astype(f32), axis=0).astype(bf)
    total = lax.all_to_all(jnp.broadcast_to(total[None], (N_TP, SPAN, 2 * HD)), "tp", 0, 0, tiled=True)
    grad_x, out_b, grad_qb = unproject(
        total.reshape(KVH, ROWS, 2 * HD), weight, out_b, grad_qb
    )
    return out_a[None], out_b[None], grad_qa[None], grad_qb[None], grad_x[None]


def solution(mesh):
    split = P("section", "ctx", "tp")
    return jax.shard_map(
        on_device,
        mesh=mesh,
        in_specs=(split, P("section", "tp", None), split, split, split, split, P()),
        out_specs=(split,) * 5,
        check_vma=False,
    )
```

```python
import math

import jax
import jax.numpy as jnp
from jax import lax
from jax.experimental import pallas as pl
from jax.experimental.pallas import tpu as pltpu
from jax.sharding import PartitionSpec as P

HEADS = 32
KVH = 4
HD = 128
SPAN = 64
N_SECTION = 2
N_Y = 8
N_Z = 4
N_CTX = 32
N_X = 4
N_CORE = 2
N_TP = 8
KEYS = N_CTX * SPAN * 2
ROWS = 128
HPD = 4
QROWS = HPD * ROWS
ALLROWS = 2 * QROWS
CHUNK = 512
NCHUNK = KEYS // CHUNK
EVERY = ("section", "ctx", "tp")
SCALE = HD ** (-0.5)
SCALE2 = SCALE * math.log2(math.e)
MIB = 1024 * 1024


def device_index(section, y, z, x, core):
    return (section * N_CTX + y * N_Z + z) * N_TP + x * N_CORE + core


def fold(u, w):
    return u + w * (N_Y - 1 - 2 * u)


def wide_groups():
    groups = []
    for section in range(N_SECTION):
        for x in range(N_X):
            for u in range(4):
                groups.append(
                    [device_index(section, fold(u, w), z, x, 0) for w in range(2) for z in range(N_Z)]
                )
            for z in range(N_Z):
                groups.append([device_index(section, y, z, x, 1) for y in range(N_Y)])
    return groups


def narrow_groups():
    groups = []
    for section in range(N_SECTION):
        for x in range(N_X):
            for w in range(2):
                for z in range(N_Z):
                    groups.append([device_index(section, fold(u, w), z, x, 0) for u in range(4)])
            for y in range(N_Y):
                groups.append([device_index(section, y, z, x, 1) for z in range(N_Z)])
    return groups


def block_owner(core):
    block = jnp.arange(N_CTX, dtype=jnp.int32)
    first, second = block // 8, block % 8
    owner_0 = fold(first, second // 4) * N_Z + second % 4
    owner_1 = second * N_Z + first
    return jnp.where(core == 0, owner_0, owner_1)


def swap_core(value):
    return lax.ppermute(value, "tp", [(i, i ^ 1) for i in range(N_TP)])


def mirror(ctx):
    return ctx - ctx % N_Z + N_Z - 1 - ctx % N_Z


def swap_section(value):
    pairs = [
        (section * N_CTX + ctx, (1 - section) * N_CTX + mirror(ctx))
        for section in range(N_SECTION)
        for ctx in range(N_CTX)
    ]
    return lax.ppermute(value, ("section", "ctx"), pairs)


def exchange(value, groups):
    return lax.all_to_all(value, EVERY, 0, 0, axis_index_groups=groups, tiled=True)


def project_kernel(x_ref, w_ref, o_ref):
    for g in range(KVH):
        o_ref[g] = nn(x_ref[...], w_ref[:, g * 2 * HD : (g + 1) * 2 * HD])


def project(features, weight):
    whole = pl.BlockSpec(memory_space=pltpu.VMEM)
    return pl.pallas_call(
        project_kernel,
        in_specs=[whole] * 2,
        out_specs=whole,
        out_shape=jax.ShapeDtypeStruct((KVH, ROWS, 2 * HD), jnp.float32),
        compiler_params=pltpu.CompilerParams(vmem_limit_bytes=16 * MIB),
        name="kv_project",
    )(features, weight)


def unproject_kernel(g_ref, w_ref, back_ref, o_ref, a_out, b_out):
    a_out[...] = back_ref[:, :QROWS]
    b_out[...] = back_ref[:, QROWS:]
    total = nt(g_ref[0], w_ref[:, : 2 * HD])
    for g in range(1, KVH):
        total += nt(g_ref[g], w_ref[:, g * 2 * HD : (g + 1) * 2 * HD])
    o_ref[...] = total.astype(jnp.bfloat16)


def unproject(kv_grads, weight, back):
    whole = pl.BlockSpec(memory_space=pltpu.VMEM)
    return pl.pallas_call(
        unproject_kernel,
        in_specs=[whole] * 3,
        out_specs=[whole] * 3,
        out_shape=[
            jax.ShapeDtypeStruct((ROWS, weight.shape[0]), jnp.bfloat16),
            jax.ShapeDtypeStruct((ROWS, QROWS), jnp.bfloat16),
            jax.ShapeDtypeStruct((ROWS, QROWS), jnp.bfloat16),
        ],
        compiler_params=pltpu.CompilerParams(vmem_limit_bytes=16 * MIB),
        name="kv_unproject",
    )(kv_grads, weight, back)


def nt(a, b):
    return lax.dot_general(a, b, (((1,), (1,)), ((), ())), preferred_element_type=jnp.float32)


def nn(a, b):
    return jnp.dot(a, b, preferred_element_type=jnp.float32)


def attention_kernel(
    base_ref, qa_ref, ga_ref, moved_ref, own_ref, other_ref,
    oa_ref, gqa_ref, back_ref, gown_ref, gother_ref,
    q_s, g_s, kt_s, vt_s, s_s,
):
    for head in range(HPD):
        cols = slice(head * HD, (head + 1) * HD)
        rows_a = slice(head * ROWS, (head + 1) * ROWS)
        rows_b = slice(QROWS + head * ROWS, QROWS + (head + 1) * ROWS)
        q_s[rows_a, :] = qa_ref[:, cols]
        g_s[rows_a, :] = ga_ref[:, cols]
        q_s[rows_b, :] = moved_ref[:, cols]
        g_s[rows_b, :] = moved_ref[:, QROWS + head * HD : QROWS + (head + 1) * HD]
    queries = q_s[...]
    grads = g_s[...]

    def key_rows(c):
        ref = own_ref if c < NCHUNK // 2 else other_ref
        return ref, slice(c % (NCHUNK // 2) * CHUNK, (c % (NCHUNK // 2) + 1) * CHUNK)

    lane = lax.broadcasted_iota(jnp.int32, (1, ALLROWS), 1)
    row = lane % ROWS
    base_a = jnp.where(row < SPAN, base_ref[64], base_ref[65])
    base_b = jnp.where(row < SPAN, base_ref[66], base_ref[67])
    q_pos = jnp.where(lane < QROWS, base_a, base_b) + row % SPAN
    key_row = lax.broadcasted_iota(jnp.int32, (SPAN, ALLROWS), 0)

    top = jnp.full((8, ALLROWS), -1e30, jnp.float32)
    for c in range(NCHUNK):
        ref, rows = key_rows(c)
        start = c * CHUNK
        tile = nt(ref[rows, :HD], queries) * SCALE2
        kt_s[:, start : start + CHUNK] = ref[rows, :HD].T
        vt_s[:, start : start + CHUNK] = ref[rows, HD:].T
        for b in range(CHUNK // SPAN):
            base = base_ref[c * (CHUNK // SPAN) + b]
            part = jnp.where(key_row <= q_pos - base, tile[b * SPAN : (b + 1) * SPAN], -1e30)
            s_s[start + b * SPAN : start + (b + 1) * SPAN, :] = part
            top = jnp.maximum(top, jnp.max(part.reshape(SPAN // 8, 8, ALLROWS), axis=0))
    top = jnp.max(top, axis=0, keepdims=True)

    total = jnp.zeros((8, ALLROWS), jnp.float32)
    out = jnp.zeros((HD, ALLROWS), jnp.float32)
    for c in range(NCHUNK):
        start = c * CHUNK
        p = jnp.exp2(s_s[start : start + CHUNK, :] - top)
        total = total + jnp.sum(p.reshape(CHUNK // 8, 8, ALLROWS), axis=0)
        out = out + nn(vt_s[:, start : start + CHUNK], p.astype(jnp.bfloat16))
    inverse = 1.0 / jnp.sum(total, axis=0, keepdims=True)
    mixed = (out * inverse).astype(jnp.bfloat16).astype(jnp.float32)
    delta = jnp.sum(mixed * grads.astype(jnp.float32).T, axis=0, keepdims=True)

    grad_q = jnp.zeros((HD, ALLROWS), jnp.float32)
    for c in range(NCHUNK):
        ref, rows = key_rows(c)
        grad_ref = gown_ref if c < NCHUNK // 2 else gother_ref
        start = c * CHUNK
        p = jnp.exp2(s_s[start : start + CHUNK, :] - top) * inverse
        grad_p = nt(ref[rows, HD:], grads)
        grad_s = (p * (grad_p - delta)).astype(jnp.bfloat16)
        grad_ref[rows, HD:] = nn(p.astype(jnp.bfloat16), grads).astype(jnp.bfloat16)
        grad_ref[rows, :HD] = (nn(grad_s, queries) * SCALE).astype(jnp.bfloat16)
        grad_q = grad_q + nn(kt_s[:, start : start + CHUNK], grad_s)
    grad_q = grad_q * SCALE

    for head in range(HPD):
        cols = slice(head * HD, (head + 1) * HD)
        late_cols = slice(QROWS + head * HD, QROWS + (head + 1) * HD)
        oa_ref[:, cols] = mixed[:, cols].T.astype(jnp.bfloat16)
        gqa_ref[:, cols] = grad_q[:, cols].T.astype(jnp.bfloat16)
        back_ref[:, cols] = mixed[:, late_cols].T.astype(jnp.bfloat16)
        back_ref[:, late_cols] = grad_q[:, late_cols].T.astype(jnp.bfloat16)


def attention(bases, qa, ga, moved, own, other):
    half = KEYS // 2
    bf = jnp.bfloat16
    whole = pl.BlockSpec(memory_space=pltpu.VMEM)
    return pl.pallas_call(
        attention_kernel,
        in_specs=[pl.BlockSpec(memory_space=pltpu.SMEM)] + [whole] * 5,
        out_specs=[whole] * 5,
        out_shape=[
            jax.ShapeDtypeStruct((ROWS, QROWS), bf),
            jax.ShapeDtypeStruct((ROWS, QROWS), bf),
            jax.ShapeDtypeStruct((ROWS, ALLROWS), bf),
            jax.ShapeDtypeStruct((half, 2 * HD), bf),
            jax.ShapeDtypeStruct((half, 2 * HD), bf),
        ],
        scratch_shapes=[
            pltpu.VMEM((ALLROWS, HD), bf),
            pltpu.VMEM((ALLROWS, HD), bf),
            pltpu.VMEM((HD, KEYS), bf),
            pltpu.VMEM((HD, KEYS), bf),
            pltpu.VMEM((KEYS, ALLROWS), jnp.float32),
        ],
        compiler_params=pltpu.CompilerParams(vmem_limit_bytes=34 * MIB),
        cost_estimate=pl.CostEstimate(
            flops=24 * QROWS * KEYS * HD, bytes_accessed=6 * MIB, transcendentals=4 * QROWS * KEYS
        ),
        name="attention",
    )(bases, qa, ga, moved, own, other)


def on_device(inputs, kv_weight, queries_a, queries_b, grads_a, grads_b, span_order):
    bf, f32 = jnp.bfloat16, jnp.float32
    weight = kv_weight[0]
    core = lax.axis_index("tp") % N_CORE
    ctx = lax.axis_index("ctx")
    wide, narrow = wide_groups(), narrow_groups()

    moved = swap_section(jnp.concatenate([queries_b[0], grads_b[0]], axis=1))

    partial = project(inputs[0], weight)
    partial = lax.all_to_all(partial.reshape(N_TP, SPAN, 2 * HD), "tp", 0, 0, tiled=True)
    own = jnp.sum(partial, axis=0).astype(bf)

    own = exchange(jnp.broadcast_to(own[None], (8, SPAN, 2 * HD)), wide)
    own = exchange(jnp.broadcast_to(own[None], (4, 8, SPAN, 2 * HD)), narrow)
    own, moved = lax.optimization_barrier((own, moved))
    own = own.reshape(N_CTX * SPAN, 2 * HD)
    other = swap_core(own)

    slots = jnp.concatenate(
        [2 * block_owner(core) + core, 2 * block_owner(1 - core) + 1 - core, 2 * ctx + jnp.arange(2), 2 * mirror(ctx) + jnp.arange(2)]
    )
    bases = span_order[slots] * SPAN

    out_a, grad_qa, back, grad_own, grad_other = attention(
        bases, queries_a[0], grads_a[0], moved, own, other
    )
    back = swap_section(back)
    grad_in = swap_core(grad_other)
    total = (grad_own.astype(f32) + grad_in.astype(f32)).astype(bf)
    total = exchange(total.reshape(4, 8, SPAN, 2 * HD), narrow)
    total, back = lax.optimization_barrier((total, back))
    total = jnp.sum(total.astype(f32), axis=0).astype(bf)
    total = exchange(total, wide)
    total = jnp.sum(total.astype(f32), axis=0).astype(bf)
    total = lax.all_to_all(jnp.broadcast_to(total[None], (N_TP, SPAN, 2 * HD)), "tp", 0, 0, tiled=True)
    grad_x, out_b, grad_qb = unproject(
        total.reshape(KVH, ROWS, 2 * HD), weight, back
    )
    return out_a[None], out_b[None], grad_qa[None], grad_qb[None], grad_x[None]


def solution(mesh):
    split = P("section", "ctx", "tp")
    return jax.shard_map(
        on_device,
        mesh=mesh,
        in_specs=(split, P("section", "tp", None), split, split, split, split, P()),
        out_specs=(split,) * 5,
        check_vma=False,
    )
```

```python
import math

import jax
import jax.numpy as jnp
from jax import lax
from jax.experimental import pallas as pl
from jax.experimental.pallas import tpu as pltpu
from jax.sharding import PartitionSpec as P

HEADS = 32
KVH = 4
HD = 128
SPAN = 64
N_SECTION = 2
N_Y = 8
N_Z = 4
N_CTX = 32
N_X = 4
N_CORE = 2
N_TP = 8
KEYS = N_CTX * SPAN * 2
ROWS = 128
HPD = 4
QROWS = HPD * ROWS
ALLROWS = 2 * QROWS
CHUNK = 512
NCHUNK = KEYS // CHUNK
EVERY = ("section", "ctx", "tp")
SCALE = HD ** (-0.5)
SCALE2 = SCALE * math.log2(math.e)
MIB = 1024 * 1024


def device_index(section, y, z, x, core):
    return (section * N_CTX + y * N_Z + z) * N_TP + x * N_CORE + core


def pair_y(u, w):
    return 2 * u + w


def wide_groups():
    groups = []
    for section in range(N_SECTION):
        for x in range(N_X):
            for u in range(4):
                groups.append(
                    [device_index(section, pair_y(u, w), z, x, 0) for w in range(2) for z in range(N_Z)]
                )
            for z in range(N_Z):
                groups.append([device_index(section, y, z, x, 1) for y in range(N_Y)])
    return groups


def narrow_groups():
    groups = []
    for section in range(N_SECTION):
        for x in range(N_X):
            for w in range(2):
                for z in range(N_Z):
                    groups.append([device_index(section, pair_y(u, w), z, x, 0) for u in range(4)])
            for y in range(N_Y):
                groups.append([device_index(section, y, z, x, 1) for z in range(N_Z)])
    return groups


def block_owner(core):
    block = jnp.arange(N_CTX, dtype=jnp.int32)
    first, second = block // 8, block % 8
    owner_0 = pair_y(first, second // 4) * N_Z + second % 4
    owner_1 = second * N_Z + first
    return jnp.where(core == 0, owner_0, owner_1)


def swap_core(value):
    return lax.ppermute(value, "tp", [(i, i ^ 1) for i in range(N_TP)])


def mirror(ctx):
    return ctx - ctx % N_Z + N_Z - 1 - ctx % N_Z


def swap_section(value):
    pairs = [
        (section * N_CTX + ctx, (1 - section) * N_CTX + mirror(ctx))
        for section in range(N_SECTION)
        for ctx in range(N_CTX)
    ]
    return lax.ppermute(value, ("section", "ctx"), pairs)


def exchange(value, groups):
    return lax.all_to_all(value, EVERY, 0, 0, axis_index_groups=groups, tiled=True)


def project_kernel(x_ref, w_ref, o_ref):
    for g in range(KVH):
        o_ref[g] = nn(x_ref[...], w_ref[:, g * 2 * HD : (g + 1) * 2 * HD])


def project(features, weight):
    whole = pl.BlockSpec(memory_space=pltpu.VMEM)
    return pl.pallas_call(
        project_kernel,
        in_specs=[whole] * 2,
        out_specs=whole,
        out_shape=jax.ShapeDtypeStruct((KVH, ROWS, 2 * HD), jnp.float32),
        compiler_params=pltpu.CompilerParams(vmem_limit_bytes=16 * MIB),
        name="kv_project",
    )(features, weight)


def unproject_kernel(g_ref, w_ref, back_ref, o_ref, a_out, b_out):
    a_out[...] = back_ref[:, :QROWS]
    b_out[...] = back_ref[:, QROWS:]
    total = nt(g_ref[0], w_ref[:, : 2 * HD])
    for g in range(1, KVH):
        total += nt(g_ref[g], w_ref[:, g * 2 * HD : (g + 1) * 2 * HD])
    o_ref[...] = total.astype(jnp.bfloat16)


def unproject(kv_grads, weight, back):
    whole = pl.BlockSpec(memory_space=pltpu.VMEM)
    return pl.pallas_call(
        unproject_kernel,
        in_specs=[whole] * 3,
        out_specs=[whole] * 3,
        out_shape=[
            jax.ShapeDtypeStruct((ROWS, weight.shape[0]), jnp.bfloat16),
            jax.ShapeDtypeStruct((ROWS, QROWS), jnp.bfloat16),
            jax.ShapeDtypeStruct((ROWS, QROWS), jnp.bfloat16),
        ],
        compiler_params=pltpu.CompilerParams(vmem_limit_bytes=16 * MIB),
        name="kv_unproject",
    )(kv_grads, weight, back)


def nt(a, b):
    return lax.dot_general(a, b, (((1,), (1,)), ((), ())), preferred_element_type=jnp.float32)


def nn(a, b):
    return jnp.dot(a, b, preferred_element_type=jnp.float32)


def attention_kernel(
    base_ref, qa_ref, ga_ref, moved_ref, own_ref, other_ref,
    oa_ref, gqa_ref, back_ref, gown_ref, gother_ref,
    q_s, g_s, kt_s, vt_s, s_s,
):
    for head in range(HPD):
        cols = slice(head * HD, (head + 1) * HD)
        rows_a = slice(head * ROWS, (head + 1) * ROWS)
        rows_b = slice(QROWS + head * ROWS, QROWS + (head + 1) * ROWS)
        q_s[rows_a, :] = qa_ref[:, cols]
        g_s[rows_a, :] = ga_ref[:, cols]
        q_s[rows_b, :] = moved_ref[:, cols]
        g_s[rows_b, :] = moved_ref[:, QROWS + head * HD : QROWS + (head + 1) * HD]
    queries = q_s[...]
    grads = g_s[...]

    def key_rows(c):
        ref = own_ref if c < NCHUNK // 2 else other_ref
        return ref, slice(c % (NCHUNK // 2) * CHUNK, (c % (NCHUNK // 2) + 1) * CHUNK)

    lane = lax.broadcasted_iota(jnp.int32, (1, ALLROWS), 1)
    row = lane % ROWS
    base_a = jnp.where(row < SPAN, base_ref[64], base_ref[65])
    base_b = jnp.where(row < SPAN, base_ref[66], base_ref[67])
    q_pos = jnp.where(lane < QROWS, base_a, base_b) + row % SPAN
    key_row = lax.broadcasted_iota(jnp.int32, (SPAN, ALLROWS), 0)

    top = jnp.full((8, ALLROWS), -1e30, jnp.float32)
    for c in range(NCHUNK):
        ref, rows = key_rows(c)
        start = c * CHUNK
        tile = nt(ref[rows, :HD], queries) * SCALE2
        kt_s[:, start : start + CHUNK] = ref[rows, :HD].T
        vt_s[:, start : start + CHUNK] = ref[rows, HD:].T
        for b in range(CHUNK // SPAN):
            base = base_ref[c * (CHUNK // SPAN) + b]
            part = jnp.where(key_row <= q_pos - base, tile[b * SPAN : (b + 1) * SPAN], -1e30)
            s_s[start + b * SPAN : start + (b + 1) * SPAN, :] = part
            top = jnp.maximum(top, jnp.max(part.reshape(SPAN // 8, 8, ALLROWS), axis=0))
    top = jnp.max(top, axis=0, keepdims=True)

    total = jnp.zeros((8, ALLROWS), jnp.float32)
    out = jnp.zeros((HD, ALLROWS), jnp.float32)
    for c in range(NCHUNK):
        start = c * CHUNK
        p = jnp.exp2(s_s[start : start + CHUNK, :] - top)
        total = total + jnp.sum(p.reshape(CHUNK // 8, 8, ALLROWS), axis=0)
        out = out + nn(vt_s[:, start : start + CHUNK], p.astype(jnp.bfloat16))
    inverse = 1.0 / jnp.sum(total, axis=0, keepdims=True)
    mixed = (out * inverse).astype(jnp.bfloat16).astype(jnp.float32)
    delta = jnp.sum(mixed * grads.astype(jnp.float32).T, axis=0, keepdims=True)

    grad_q = jnp.zeros((HD, ALLROWS), jnp.float32)
    for c in range(NCHUNK):
        ref, rows = key_rows(c)
        grad_ref = gown_ref if c < NCHUNK // 2 else gother_ref
        start = c * CHUNK
        p = jnp.exp2(s_s[start : start + CHUNK, :] - top) * inverse
        grad_p = nt(ref[rows, HD:], grads)
        grad_s = (p * (grad_p - delta)).astype(jnp.bfloat16)
        grad_ref[rows, HD:] = nn(p.astype(jnp.bfloat16), grads).astype(jnp.bfloat16)
        grad_ref[rows, :HD] = (nn(grad_s, queries) * SCALE).astype(jnp.bfloat16)
        grad_q = grad_q + nn(kt_s[:, start : start + CHUNK], grad_s)
    grad_q = grad_q * SCALE

    for head in range(HPD):
        cols = slice(head * HD, (head + 1) * HD)
        late_cols = slice(QROWS + head * HD, QROWS + (head + 1) * HD)
        oa_ref[:, cols] = mixed[:, cols].T.astype(jnp.bfloat16)
        gqa_ref[:, cols] = grad_q[:, cols].T.astype(jnp.bfloat16)
        back_ref[:, cols] = mixed[:, late_cols].T.astype(jnp.bfloat16)
        back_ref[:, late_cols] = grad_q[:, late_cols].T.astype(jnp.bfloat16)


def attention(bases, qa, ga, moved, own, other):
    half = KEYS // 2
    bf = jnp.bfloat16
    whole = pl.BlockSpec(memory_space=pltpu.VMEM)
    return pl.pallas_call(
        attention_kernel,
        in_specs=[pl.BlockSpec(memory_space=pltpu.SMEM)] + [whole] * 5,
        out_specs=[whole] * 5,
        out_shape=[
            jax.ShapeDtypeStruct((ROWS, QROWS), bf),
            jax.ShapeDtypeStruct((ROWS, QROWS), bf),
            jax.ShapeDtypeStruct((ROWS, ALLROWS), bf),
            jax.ShapeDtypeStruct((half, 2 * HD), bf),
            jax.ShapeDtypeStruct((half, 2 * HD), bf),
        ],
        scratch_shapes=[
            pltpu.VMEM((ALLROWS, HD), bf),
            pltpu.VMEM((ALLROWS, HD), bf),
            pltpu.VMEM((HD, KEYS), bf),
            pltpu.VMEM((HD, KEYS), bf),
            pltpu.VMEM((KEYS, ALLROWS), jnp.float32),
        ],
        compiler_params=pltpu.CompilerParams(vmem_limit_bytes=34 * MIB),
        cost_estimate=pl.CostEstimate(
            flops=24 * QROWS * KEYS * HD, bytes_accessed=6 * MIB, transcendentals=4 * QROWS * KEYS
        ),
        name="attention",
    )(bases, qa, ga, moved, own, other)


def on_device(inputs, kv_weight, queries_a, queries_b, grads_a, grads_b, span_order):
    bf, f32 = jnp.bfloat16, jnp.float32
    weight = kv_weight[0]
    core = lax.axis_index("tp") % N_CORE
    ctx = lax.axis_index("ctx")
    wide, narrow = wide_groups(), narrow_groups()

    moved = swap_section(jnp.concatenate([queries_b[0], grads_b[0]], axis=1))

    partial = project(inputs[0], weight)
    partial = lax.all_to_all(partial.reshape(N_TP, SPAN, 2 * HD), "tp", 0, 0, tiled=True)
    own = jnp.sum(partial, axis=0).astype(bf)

    own = exchange(jnp.broadcast_to(own[None], (8, SPAN, 2 * HD)), wide)
    own = exchange(jnp.broadcast_to(own[None], (4, 8, SPAN, 2 * HD)), narrow)
    own, moved = lax.optimization_barrier((own, moved))
    own = own.reshape(N_CTX * SPAN, 2 * HD)
    other = swap_core(own)

    slots = jnp.concatenate(
        [2 * block_owner(core) + core, 2 * block_owner(1 - core) + 1 - core, 2 * ctx + jnp.arange(2), 2 * mirror(ctx) + jnp.arange(2)]
    )
    bases = span_order[slots] * SPAN

    out_a, grad_qa, back, grad_own, grad_other = attention(
        bases, queries_a[0], grads_a[0], moved, own, other
    )
    back = swap_section(back)
    grad_in = swap_core(grad_other)
    total = (grad_own.astype(f32) + grad_in.astype(f32)).astype(bf)
    total = exchange(total.reshape(4, 8, SPAN, 2 * HD), narrow)
    total, back = lax.optimization_barrier((total, back))
    total = jnp.sum(total.astype(f32), axis=0).astype(bf)
    total = exchange(total, wide)
    total = jnp.sum(total.astype(f32), axis=0).astype(bf)
    total = lax.all_to_all(jnp.broadcast_to(total[None], (N_TP, SPAN, 2 * HD)), "tp", 0, 0, tiled=True)
    grad_x, out_b, grad_qb = unproject(
        total.reshape(KVH, ROWS, 2 * HD), weight, back
    )
    return out_a[None], out_b[None], grad_qa[None], grad_qb[None], grad_x[None]


def solution(mesh):
    split = P("section", "ctx", "tp")
    return jax.shard_map(
        on_device,
        mesh=mesh,
        in_specs=(split, P("section", "tp", None), split, split, split, split, P()),
        out_specs=(split,) * 5,
        check_vma=False,
    )
```
